32 devices in a mesh: tm: 4 (over z), sx: 4 (over y, x), sy: 2 (over core).
Axes of the slice: x: 2, y: 2, z: 4, core: 2. Of those that a mesh axis runs over, the one named last changes fastest.
Arguments:
- sources: float32 [8, 32, 32, 128], P('tm', 'sx', 'sy'), may hold values from -6 to 6
- forward_states: float32 [8, 32, 32, 128], P('tm', 'sx', 'sy'), may hold values from -6 to 6
- terminal: float32 [32, 32, 128], P('sx', 'sy'), may hold values from -6 to 6
- damping: float32 [32, 32, 128], P('sx', 'sy'), may hold values from 0.001 to 0.1
- contact_stiff: float32 [8], replicated, may hold values from 0.001 to 1
- regions: int32 [8, 4, 4], P('tm', 'sx', 'sy'), may hold values from 0 to 7
Outputs:
- adjoint: float32 [8, 32, 32, 128], P('tm', 'sx', 'sy')
- damping_grad: float32 [32, 32, 128], P('sx', 'sy')
The draws below stay inside these ranges and needn't reach their ends.
Inputs may be any that keep to these rules, and one draw needn't show every extreme that they name: `regions`: region of a block of 8 x 8 columns of cells at a step.
All inputs are finite; a program needn't handle non-finite values.
Results may differ from the reference program's by a relative error of at most 0.0003.
Values sent between devices are 32-bit elements; how exact they have to be, the bound alone decides.
A program may use at most 64 MiB of HBM per device.

```python
import math
import jax
import jax.numpy as jnp
import numpy as np
from jax import lax

CZ = 128
STEPS_DEV = 2
SWEEPS = 4
REGIONS = 8
BLOCK_CELLS = 8
NX = 32
NY = 32
NT = 8
N_TM = 4


def place_ends(result, stream_key, low, high):
    dims = result.shape
    place = [jax.random.randint(jax.random.fold_in(stream_key, axis), (), 0, dims[axis]) for axis in range(len(dims))]
    result = result.at[tuple(place)].set(low)
    longest = dims.index(max(dims))
    place[longest] = (place[longest] + 1) % dims[longest]
    return result.at[tuple(place)].set(high)


def block_scale(own_key, shape, shards, least, largest):
    def one(dim, parts):
        heights = jax.random.uniform(jax.random.fold_in(jax.random.fold_in(own_key, 6), dim), (parts,), jnp.float32, least / len(shards), largest / len(shards))
        return jnp.repeat(jnp.exp(heights), shape[dim] // parts).reshape((-1,) + (1,) * (len(shape) - dim - 1))

    level = one(*shards[0])
    for cut in shards[1:]:
        level = level * one(*cut)
    return level


def rank_bounds(number_of, lean):
    weights = [(1 << 20) // math.isqrt(rank ** lean) + 1 for rank in range(1, number_of + 1)]
    width = 1 + sum(weights) // (1 << 30)
    return np.cumsum(np.array([max(1, weight // width) for weight in weights]))


def skewed_ids(stream_key, shape, count, lean):
    table = rank_bounds(count, lean)
    ticket = jax.random.randint(jax.random.fold_in(stream_key, 1), shape, 0, int(table[count - 1]))
    standing = jnp.searchsorted(jnp.asarray(table, jnp.int32), ticket, side="right")
    return jax.random.permutation(jax.random.fold_in(stream_key, 2), count)[standing].astype(jnp.int32)


def gaussian(key, shape, scale, reach, shards=(), kind=jnp.bfloat16):
    values = scale * jax.random.normal(key, shape, jnp.float32)
    if shards:
        values = values * block_scale(key, shape, shards, -0.22, 0.18)
    return jnp.clip(values, -reach, reach).astype(kind)


def setup_inputs(seed: int = 0) -> dict:
    streams_of = jax.random.split(jax.random.key(seed), 7)
    sources = gaussian(streams_of[0], (NT, NX, NY, CZ), 1.0, 6.0, ((0, 4), (1, 4), (2, 2)), jnp.float32)
    forward_states = gaussian(streams_of[1], (NT, NX, NY, CZ), 1.0, 6.0, ((0, 4), (1, 4), (2, 2)), jnp.float32)
    terminal = gaussian(streams_of[2], (NX, NY, CZ), 1.0, 6.0, ((0, 4), (1, 2)), jnp.float32)
    damping = jnp.clip(jnp.exp(math.log(0.1) - 4.6051702 * jax.random.uniform(streams_of[3], (NX, NY, CZ), jnp.float32) ** block_scale(streams_of[3], (NX, NY, CZ), ((0, 4), (1, 2)), -0.2, 0.2)), 0.001, 0.1)
    contact_stiff = jnp.clip(jnp.exp(jax.random.uniform(streams_of[4], (REGIONS,), jnp.float32, math.log(0.001), math.log(1.0))), 0.001, 1.0)
    regions = place_ends(skewed_ids(streams_of[5], (NT, NX // BLOCK_CELLS, NY // BLOCK_CELLS), REGIONS, 2), jax.random.fold_in(streams_of[5], 3), 0, REGIONS - 1).astype(jnp.int32)
    return dict(sources=sources, forward_states=forward_states, terminal=terminal, damping=damping, contact_stiff=contact_stiff, regions=regions)


coupling = 0.5


def neighbours(field):
    padded = jnp.pad(field, 1)
    total = padded[2:, 1:-1, 1:-1] + padded[:-2, 1:-1, 1:-1]
    total = total + padded[1:-1, 2:, 1:-1] + padded[1:-1, :-2, 1:-1]
    total = total + padded[1:-1, 1:-1, 2:] + padded[1:-1, 1:-1, :-2]
    return total


def propagate(right, diagonal):
    field = right
    for sweep_index in range(SWEEPS):
        field = (right + coupling * neighbours(field)) / diagonal
    return field


def reaction(region_ids, contact_stiff, damping):
    labels = jnp.arange(REGIONS, dtype=jnp.int32)
    picked = jnp.sum(jnp.where(region_ids[:, :, None] == labels, contact_stiff, jnp.zeros_like(contact_stiff)), axis=2)
    spread = jnp.repeat(jnp.repeat(picked, BLOCK_CELLS, axis=0), BLOCK_CELLS, axis=1)
    return spread[:, :, None] + damping


def reference(sources, forward_states, terminal, damping, contact_stiff, regions):
    grid = damping.shape
    slab_src = sources.reshape((N_TM, STEPS_DEV) + grid)
    slab_states = forward_states.reshape((N_TM, STEPS_DEV) + grid)
    slab_reg = regions.reshape((N_TM, STEPS_DEV) + regions.shape[1:])
    slab_ids = jnp.arange(N_TM, dtype=jnp.int32)

    def first_pass(inputs):
        src_here, reg_here, slab_index = inputs
        field = jnp.where(slab_index == N_TM - 1, terminal, jnp.zeros_like(terminal))
        for position in range(STEPS_DEV - 1, -1, -1):
            diagonal = 1.0 + reaction(reg_here[position], contact_stiff, damping) + 6.0 * coupling
            field = propagate(field, diagonal) + src_here[position]
        return field

    coarse_rhs = lax.map(first_pass, (slab_src, slab_reg, slab_ids))

    def coarse_factor(region_first):
        return 1.0 / (1.0 + STEPS_DEV * reaction(region_first, contact_stiff, damping))

    factors = lax.map(coarse_factor, slab_reg[:, 0])

    def advance(carry, inputs):
        factor, rhs = inputs
        value = factor * carry + rhs
        return value, value

    final_carry, corrected = lax.scan(advance, jnp.zeros_like(terminal), (factors, coarse_rhs), reverse=True)
    incoming = jnp.concatenate([corrected[1:], terminal[None]], axis=0)

    def final_pass(inputs):
        src_here, reg_here, states_here, field, head = inputs
        layers = [head] + [head] * (STEPS_DEV - 1)
        for position in range(STEPS_DEV - 1, 0, -1):
            diagonal = 1.0 + reaction(reg_here[position], contact_stiff, damping) + 6.0 * coupling
            field = propagate(field, diagonal) + src_here[position]
            layers[position] = field
        stacked = jnp.stack(layers)
        return stacked, jnp.sum(stacked * states_here, axis=0)

    adjoint, partials = lax.map(final_pass, (slab_src, slab_reg, slab_states, incoming, corrected))
    damping_grad = -jnp.sum(partials, axis=0)
    return adjoint.reshape(sources.shape), damping_grad
```

```python
import functools

import jax
import jax.numpy as jnp
from jax import lax
from jax.experimental import pallas as pl
from jax.experimental.pallas import tpu as pltpu
from jax.sharding import PartitionSpec as P

MESH = pl.DeviceIdType.MESH
SWEEPS = 4
BLOCK_CELLS = 8
COUPLING = 0.5
H = SWEEPS
HY = 8

XLO, XHI, YS, CLO, CHI, MAIN0, MAIN1 = range(7)


def kernel(
    nt, ns, src_ref, fs_ref, term_ref, damp_ref, stiff_ref, reg_ref,
    adj_ref, grad_ref,
    g, m, xa, xb, c, r, p, tot,
    g_send, g_recv, h_send, h_recv, u_send, m_send, m_recv, r_send, r_recv, t_send, t_recv,
):
    steps, bx, by, cz = src_ref.shape
    ex, ey = bx + 2 * H, by + HY
    t = lax.axis_index("tm")
    sx = lax.axis_index("sx")
    sy = lax.axis_index("sy")
    last = t == nt - 1
    other = 1 - sy
    has_lo, has_hi = sx > 0, sx < ns - 1
    always = t >= 0
    ys = pl.multiple_of(other * HY, HY)

    core = pl.ds(0, by)
    edge = pl.ds(ys, HY)
    far = pl.ds(by, HY)
    pieces = [
        (XHI, has_lo, sx - 1, sy, (0, H), H + bx, core, core),
        (XLO, has_hi, sx + 1, sy, (bx - H, bx), 0, core, core),
        (YS, always, sx, other, (0, bx), H, edge, far),
        (CHI, has_lo, sx - 1, other, (0, H - 1), H + bx, edge, far),
        (CLO, has_hi, sx + 1, other, (bx - H + 1, bx), 1, edge, far),
    ]
    arrives = {XLO: has_lo, XHI: has_hi, YS: always, CLO: has_lo, CHI: has_hi}

    zero = jnp.zeros((ex, ey, cz), jnp.float32)
    for field in range(3):
        g[field] = zero
    m[...] = zero

    barrier = pltpu.get_barrier_semaphore()

    def greet(cond, dev):
        @pl.when(cond)
        def _():
            pl.semaphore_signal(barrier, inc=1, device_id=dev, device_id_type=MESH)

    for slot, cond, dx, dy, *_ in pieces:
        greet(cond, (t, dx, dy))
    for dt, cond_t in ((t - 1, t > 0), (t + 1, t < nt - 1)):
        greet(cond_t, (dt, sx, sy))
        for slot, cond, dx, dy, *_ in pieces:
            greet(jnp.logical_and(cond_t, cond), (dt, dx, dy))
    greet(t >= 2, (0, sx, sy))
    for k in range(2, nt):
        greet(t == 0, (k, sx, sy))
    one = lambda cond: jnp.where(cond, 1, 0)
    around = 2 * (one(has_lo) + one(has_hi)) + 1
    slabs = one(t > 0) + one(t < nt - 1)
    friends = around + slabs * (around + 1) + one(t >= 2) + one(t == 0) * (nt - 2)

    def reaction(step):
        columns = []
        for j in range(by // BLOCK_CELLS):
            rows = slice(j * BLOCK_CELLS, (j + 1) * BLOCK_CELLS)
            parts = []
            for i in range(bx // BLOCK_CELLS):
                cells = slice(i * BLOCK_CELLS, (i + 1) * BLOCK_CELLS)
                parts.append(damp_ref[cells, rows, :] + stiff_ref[reg_ref[step, i, j]])
            columns.append(jnp.concatenate(parts, axis=0) if len(parts) > 1 else parts[0])
        return jnp.concatenate(columns, axis=1)

    react_lo, react_hi = reaction(0), reaction(1)
    inv_lo = 1.0 / (1.0 + react_lo + 6.0 * COUPLING)
    inv_hi = 1.0 / (1.0 + react_hi + 6.0 * COUPLING)
    factor = 1.0 / (1.0 + steps * react_lo)
    c[...] = factor
    body = pl.ds(H, bx)
    g[0, body, core, :] = jnp.where(last, term_ref[...], src_ref[1])
    g[1, body, core, :] = jnp.where(last, inv_hi, inv_lo)
    g[2, body, core, :] = jnp.where(last, inv_lo, inv_hi)

    def piece_copy(piece, src, off, dst, dt, send, recv, fields=None):
        slot, cond, dx, dy, (lo, hi), to, ysrc, ydst = piece
        s_at = (pl.ds(off + lo, hi - lo), ysrc)
        d_at = (pl.ds(to, hi - lo), ydst)
        if fields is not None:
            s_at, d_at = (fields,) + s_at, (fields,) + d_at
        return pltpu.make_async_remote_copy(
            src_ref=src.at[s_at], dst_ref=dst.at[d_at],
            send_sem=send.at[slot], recv_sem=recv.at[slot],
            device_id=(dt, dx, dy), device_id_type=MESH,
        )

    def start(cond, copy):
        @pl.when(cond)
        def _():
            copy.start()

    def wait_in(cond, copy):
        @pl.when(cond)
        def _():
            copy.wait_recv()

    def wait_out(cond, copy):
        @pl.when(cond)
        def _():
            copy.wait_send()

    first = [(q, piece_copy(q, g, H, g, t, g_send, g_recv, pl.ds(0, 2))) for q in pieces]
    second = [(q, piece_copy(q, g, H, g, t, h_send, h_recv, pl.ds(2, 1))) for q in pieces]
    around_m = [(q, piece_copy(q, m, H, m, t, u_send, m_recv)) for q in pieces]
    down = [(q, piece_copy(q, c, 0, m, t - 1, m_send, m_recv)) for q in pieces]
    half = bx // 2
    mains = [
        pltpu.make_async_remote_copy(
            src_ref=c.at[pl.ds(i * half, half)], dst_ref=m.at[pl.ds(H + i * half, half), core],
            send_sem=m_send.at[MAIN0 + i], recv_sem=m_recv.at[MAIN0 + i],
            device_id=(t - 1, sx, sy), device_id_type=MESH,
        )
        for i in range(2)
    ]

    pl.semaphore_wait(barrier, friends)
    for q, copy in first:
        start(q[1], copy)
    for q, copy in second:
        start(q[1], copy)

    lane = lax.broadcasted_iota(jnp.int32, (ey, cz), 1)
    row = lax.broadcasted_iota(jnp.int32, (ey, cz), 0)
    no_before = jnp.logical_and(row == 0, sy == 0)
    no_after = jnp.logical_and(row == by - 1, sy == 1)
    z_first, z_last = lane == 0, lane == cz - 1

    def phi(b, inv):
        bufs = [b, xa, xb]
        cur = b
        out = []
        for s in range(1, SWEEPS + 1):
            nxt = xa if s % 2 else xb
            for i in range(s, ex - s):
                x = cur[i]
                total = cur[i - 1] + cur[i + 1]
                total += jnp.where(no_before, 0.0, pltpu.roll(x, 1, 0))
                total += jnp.where(no_after, 0.0, pltpu.roll(x, ey - 1, 0))
                total += jnp.where(z_first, 0.0, pltpu.roll(x, 1, 1))
                total += jnp.where(z_last, 0.0, pltpu.roll(x, cz - 1, 1))
                value = (b[i] + COUPLING * total) * inv[i]
                if s == SWEEPS:
                    out.append(value[:by])
                else:
                    nxt[i] = value
            cur = nxt
        return out

    def arrived(copies):
        for q, copy in copies:
            wait_in(arrives[q[0]], copy)

    arrived(first)
    y1 = phi(g.at[0], g.at[1])
    arrived(second)

    @pl.when(last)
    def _():
        for i in range(bx):
            value = y1[i] + src_ref[1, i]
            adj_ref[1, i] = value
            m[H + i, core, :] = value
        for q, copy in around_m:
            start(q[1], copy)
        arrived(around_m)
        top = phi(m, g.at[2])
        for i in range(bx):
            c[i] = top[i] + src_ref[0, i]

    not_last = jnp.logical_not(last)

    @pl.when(not_last)
    def _():
        for i in range(bx):
            adj_ref[0, i] = y1[i] + src_ref[0, i]

    def send_half(i):
        start(t > 0, mains[i])
        for q, copy in down:
            if q[0] in ((XHI, CHI) if i == 0 else (XLO, CLO, YS)):
                start(jnp.logical_and(t > 0, q[1]), copy)

    for i in range(2):
        rows = pl.ds(i * half, half)

        @pl.when(not_last)
        def _():
            mains[i].wait_recv()
            c[rows] = c[rows] * m[pl.ds(H + i * half, half), core, :] + adj_ref[0, rows]

        send_half(i)
    adj_ref[0] = c[...]

    @pl.when(not_last)
    def _():
        arrived(down)
        top = phi(m, g.at[2])
        for i in range(bx):
            adj_ref[1, i] = top[i] + src_ref[1, i]

    p[...] = -(adj_ref[0] * fs_ref[0] + adj_ref[1] * fs_ref[1])
    to_prev = pltpu.make_async_remote_copy(
        src_ref=p, dst_ref=r, send_sem=r_send.at[0], recv_sem=r_recv.at[0],
        device_id=(t - 1, sx, sy), device_id_type=MESH,
    )
    spread = [
        pltpu.make_async_remote_copy(
            src_ref=p, dst_ref=tot, send_sem=t_send.at[k], recv_sem=t_recv.at[0],
            device_id=(k, sx, sy), device_id_type=MESH,
        )
        for k in range(1, nt)
    ]

    @pl.when(not_last)
    def _():
        to_prev.wait_recv()
        p[...] += r[...]

    @pl.when(t > 0)
    def _():
        to_prev.start()
        spread[0].wait_recv()
        grad_ref[...] = tot[...]
        to_prev.wait_send()
        for copy in mains:
            copy.wait_send()

    @pl.when(t == 0)
    def _():
        for copy in spread:
            copy.start()
        grad_ref[...] = p[...]
        for copy in spread:
            copy.wait_send()

    for q, copy in first + second:
        wait_out(q[1], copy)
    for q, copy in around_m:
        wait_out(jnp.logical_and(last, q[1]), copy)
    for q, copy in down:
        wait_out(jnp.logical_and(t > 0, q[1]), copy)


def shards(sources, forward_states, terminal, damping, contact_stiff, regions):
    nt, ns = lax.axis_size("tm"), lax.axis_size("sx")
    steps, bx, by, cz = sources.shape
    assert steps == 2 and lax.axis_size("sy") == 2
    vmem = pl.BlockSpec(memory_space=pltpu.VMEM)
    smem = pl.BlockSpec(memory_space=pltpu.SMEM)
    f32 = jnp.float32
    ext = (bx + 2 * H, by + HY, cz)
    block = (bx, by, cz)
    dma = pltpu.SemaphoreType.DMA
    return pl.pallas_call(
        functools.partial(kernel, nt, ns),
        out_shape=(
            jax.ShapeDtypeStruct(sources.shape, f32),
            jax.ShapeDtypeStruct(block, f32),
        ),
        in_specs=[vmem] * 4 + [smem] * 2,
        out_specs=(vmem, vmem),
        scratch_shapes=[
            pltpu.VMEM((3,) + ext, f32),
            pltpu.VMEM(ext, f32),
            pltpu.VMEM(ext, f32),
            pltpu.VMEM(ext, f32),
            pltpu.VMEM(block, f32),
            pltpu.VMEM(block, f32),
            pltpu.VMEM(block, f32),
            pltpu.VMEM(block, f32),
            dma((5,)), dma((5,)), dma((5,)), dma((5,)), dma((5,)),
            dma((7,)), dma((7,)), dma((1,)), dma((1,)), dma((nt,)), dma((1,)),
        ],
        compiler_params=pltpu.CompilerParams(
            collective_id=0, has_side_effects=True, vmem_limit_bytes=32 * 1024 * 1024
        ),
    )(sources, forward_states, terminal, damping, contact_stiff, regions)


def solution(mesh):
    in_specs = (
        P("tm", "sx", "sy", None),
        P("tm", "sx", "sy", None),
        P("sx", "sy", None),
        P("sx", "sy", None),
        P(),
        P("tm", "sx", "sy"),
    )
    out_specs = (P("tm", "sx", "sy", None), P("sx", "sy", None))
    return jax.shard_map(shards, mesh=mesh, in_specs=in_specs, out_specs=out_specs, check_vma=False)
```

```python
import functools

import jax
import jax.numpy as jnp
from jax import lax
from jax.experimental import pallas as pl
from jax.experimental.pallas import tpu as pltpu
from jax.sharding import PartitionSpec as P

MESH = pl.DeviceIdType.MESH
SWEEPS = 4
BLOCK_CELLS = 8
COUPLING = 0.5
H = SWEEPS
HY = 8

XLO, XHI, YS, CLO, CHI, MAIN0, MAIN1 = range(7)


def kernel(
    nt, ns, src_hbm, fs_hbm, term_hbm, damp_hbm, stiff_hbm, reg_hbm,
    adj_ref, grad_ref,
    src_ref, fs_ref, stiff_ref, reg_ref, picks, inv,
    g, m, xa, xb, c, r, p, tot,
    l_sem, g_send, g_recv, h_send, h_recv, u_send, m_send, m_recv, r_send, r_recv, t_send, t_recv,
):
    steps, bx, by, cz = src_ref.shape
    ex, ey = bx + 2 * H, by + HY
    t = lax.axis_index("tm")
    sx = lax.axis_index("sx")
    sy = lax.axis_index("sy")
    last = t == nt - 1
    other = 1 - sy
    has_lo, has_hi = sx > 0, sx < ns - 1
    always = t >= 0
    ys = pl.multiple_of(other * HY, HY)

    core = pl.ds(0, by)
    edge = pl.ds(ys, HY)
    far = pl.ds(by, HY)
    pieces = [
        (XHI, has_lo, sx - 1, sy, (0, H), H + bx, core, core),
        (XLO, has_hi, sx + 1, sy, (bx - H, bx), 0, core, core),
        (YS, always, sx, other, (0, bx), H, edge, far),
        (CHI, has_lo, sx - 1, other, (0, H - 1), H + bx, edge, far),
        (CLO, has_hi, sx + 1, other, (bx - H + 1, bx), 1, edge, far),
    ]
    arrives = {XLO: has_lo, XHI: has_hi, YS: always, CLO: has_lo, CHI: has_hi}

    body = pl.ds(H, bx)
    own = g.at[0, body, core]
    loads = [
        pltpu.make_async_copy(stiff_hbm, stiff_ref, l_sem.at[0]),
        pltpu.make_async_copy(reg_hbm, reg_ref, l_sem.at[1]),
        pltpu.make_async_copy(damp_hbm, g.at[1, body, core], l_sem.at[2]),
        pltpu.make_async_copy(src_hbm, src_ref, l_sem.at[3]),
        pltpu.make_async_copy(fs_hbm, fs_ref, l_sem.at[4]),
    ]
    from_term = pltpu.make_async_copy(term_hbm, own, l_sem.at[5])
    from_src = pltpu.make_async_copy(src_hbm.at[1], own, l_sem.at[5])
    for load in loads[:3]:
        load.start()

    @pl.when(t == nt - 1)
    def _():
        from_term.start()

    @pl.when(t != nt - 1)
    def _():
        from_src.start()

    for load in loads[3:]:
        load.start()

    edge_zero = jnp.zeros((H, ey, cz), jnp.float32)
    far_zero = jnp.zeros((bx, HY, cz), jnp.float32)
    for ref in (g.at[0], g.at[1], m):
        ref[0:H] = edge_zero
        ref[H + bx : ex] = edge_zero
        ref[H : H + bx, by:ey] = far_zero

    barrier = pltpu.get_barrier_semaphore()

    def greet(cond, dev):
        @pl.when(cond)
        def _():
            pl.semaphore_signal(barrier, inc=1, device_id=dev, device_id_type=MESH)

    for slot, cond, dx, dy, *_ in pieces:
        greet(cond, (t, dx, dy))
    for dt, cond_t in ((t - 1, t > 0), (t + 1, t < nt - 1)):
        greet(cond_t, (dt, sx, sy))
        for slot, cond, dx, dy, *_ in pieces:
            greet(jnp.logical_and(cond_t, cond), (dt, dx, dy))
    greet(t >= 2, (0, sx, sy))
    for k in range(2, nt):
        greet(t == 0, (k, sx, sy))
    one = lambda cond: jnp.where(cond, 1, 0)
    around = 2 * (one(has_lo) + one(has_hi)) + 1
    slabs = one(t > 0) + one(t < nt - 1)
    friends = around + slabs * (around + 1) + one(t >= 2) + one(t == 0) * (nt - 2)

    blocks = by // BLOCK_CELLS
    for load in loads[:2]:
        load.wait()
    late = jnp.where(t == nt - 1, 1, 0)
    for j in range(blocks):
        for k, step in enumerate((late, 1 - late)):
            value = stiff_ref[reg_ref[step, 0, j]]
            picks[5, j * steps + k : j * steps + k + 1, :] = jnp.full((1, cz), value, jnp.float32)

    def piece_copy(piece, src, off, dst, dt, send, recv, fields=None):
        slot, cond, dx, dy, (lo, hi), to, ysrc, ydst = piece
        s_at = (pl.ds(off + lo, hi - lo), ysrc)
        d_at = (pl.ds(to, hi - lo), ydst)
        if fields is not None:
            s_at, d_at = (fields,) + s_at, (fields,) + d_at
        return pltpu.make_async_remote_copy(
            src_ref=src.at[s_at], dst_ref=dst.at[d_at],
            send_sem=send.at[slot], recv_sem=recv.at[slot],
            device_id=(dt, dx, dy), device_id_type=MESH,
        )

    def start(cond, copy):
        @pl.when(cond)
        def _():
            copy.start()

    def wait_in(cond, copy):
        @pl.when(cond)
        def _():
            copy.wait_recv()

    def wait_out(cond, copy):
        @pl.when(cond)
        def _():
            copy.wait_send()

    first = [(q, piece_copy(q, g, H, g, t, g_send, g_recv, pl.ds(0, 2))) for q in pieces]
    second = [
        (
            q,
            pltpu.make_async_remote_copy(
                src_ref=picks.at[5], dst_ref=picks.at[q[0]],
                send_sem=h_send.at[q[0]], recv_sem=h_recv.at[q[0]],
                device_id=(t, q[2], q[3]), device_id_type=MESH,
            ),
        )
        for q in pieces
    ]
    around_m = [(q, piece_copy(q, m, H, m, t, u_send, m_recv)) for q in pieces]
    down = [(q, piece_copy(q, c, 0, m, t - 1, m_send, m_recv)) for q in pieces]
    chunks = 4
    half = bx // chunks
    mains = [
        pltpu.make_async_remote_copy(
            src_ref=c.at[pl.ds(i * half, half)], dst_ref=m.at[pl.ds(H + i * half, half), core],
            send_sem=m_send.at[MAIN0 + i], recv_sem=m_recv.at[MAIN0 + i],
            device_id=(t - 1, sx, sy), device_id_type=MESH,
        )
        for i in range(chunks)
    ]

    pl.semaphore_wait(barrier, friends)
    for q, copy in second:
        start(q[1], copy)
    loads[2].wait()
    from_src.wait()
    for q, copy in first:
        start(q[1], copy)

    lane = lax.broadcasted_iota(jnp.int32, (ey, cz), 1)
    row = lax.broadcasted_iota(jnp.int32, (ey, cz), 0)
    no_before = jnp.logical_and(row == 0, sy == 0)
    no_after = jnp.logical_and(row == by - 1, sy == 1)
    z_first, z_last = lane == 0, lane == cz - 1

    def phi(b, inv):
        bufs = [b, xa, xb]
        cur = b
        out = []
        for s in range(1, SWEEPS + 1):
            nxt = xa if s % 2 else xb
            for i in range(s, ex - s):
                x = cur[i]
                total = cur[i - 1] + cur[i + 1]
                total += jnp.where(no_before, 0.0, pltpu.roll(x, 1, 0))
                total += jnp.where(no_after, 0.0, pltpu.roll(x, ey - 1, 0))
                total += jnp.where(z_first, 0.0, pltpu.roll(x, 1, 1))
                total += jnp.where(z_last, 0.0, pltpu.roll(x, cz - 1, 1))
                value = (b[i] + COUPLING * total) * inv[i]
                if s == SWEEPS:
                    out.append(value[:by])
                else:
                    nxt[i] = value
            cur = nxt
        return out

    def arrived(copies):
        for q, copy in copies:
            wait_in(arrives[q[0]], copy)

    def pick(slot, j, k):
        return picks[slot, j * steps + k : j * steps + k + 1, :]

    def near_pick(slot, k):
        if blocks == 1:
            return pick(slot, 0, k)
        return jnp.where(sy == 1, pick(slot, blocks - 1, k), pick(slot, 0, k))

    def fill(out, k, rows, straight, corner, inside):
        for i in rows:
            for j in range(blocks):
                cells = slice(j * BLOCK_CELLS, (j + 1) * BLOCK_CELLS)
                value = 1.0 / (1.0 + (pick(straight, j, k) + g[1, i, cells, :]) + 6.0 * COUPLING)
                inv[out, i, cells, :] = jnp.where(inside, value, 0.0)
            value = 1.0 / (1.0 + (near_pick(corner, k) + g[1, i, by:ey, :]) + 6.0 * COUPLING)
            inv[out, i, by:ey, :] = jnp.where(inside, value, 0.0)

    def fill_all(out, k):
        fill(out, k, range(1, H), XLO, CLO, has_lo)
        fill(out, k, range(H, H + bx), 5, YS, always)
        fill(out, k, range(H + bx, ex - 1), XHI, CHI, has_hi)

    loads[3].wait()
    arrived(second)
    arrived(first)
    fill_all(0, 0)
    y1 = phi(g.at[0], inv.at[0])

    @pl.when(last)
    def _():
        for i in range(bx):
            value = y1[i] + src_ref[1, i]
            adj_ref[1, i] = value
            m[H + i, core, :] = value
        for q, copy in around_m:
            start(q[1], copy)

    fill_all(1, 1)

    @pl.when(last)
    def _():
        arrived(around_m)
        top = phi(m, inv.at[1])
        for i in range(bx):
            c[i] = top[i] + src_ref[0, i]

    not_last = jnp.logical_not(last)

    @pl.when(not_last)
    def _():
        for j in range(blocks):
            cells = slice(j * BLOCK_CELLS, (j + 1) * BLOCK_CELLS)
            c[:, cells, :] = 1.0 / (1.0 + steps * (pick(5, j, 0) + g[1, H : H + bx, cells, :]))
        for i in range(bx):
            adj_ref[0, i] = y1[i] + src_ref[0, i]

    for i in range(chunks):
        rows = pl.ds(i * half, half)

        @pl.when(not_last)
        def _():
            mains[i].wait_recv()
            c[rows] = c[rows] * m[pl.ds(H + i * half, half), core, :] + adj_ref[0, rows]

        start(t > 0, mains[i])
    for q, copy in down:
        start(jnp.logical_and(t > 0, q[1]), copy)
    adj_ref[0] = c[...]

    @pl.when(not_last)
    def _():
        arrived(down)
        top = phi(m, inv.at[1])
        for i in range(bx):
            adj_ref[1, i] = top[i] + src_ref[1, i]

    loads[4].wait()
    p[...] = -(adj_ref[0] * fs_ref[0] + adj_ref[1] * fs_ref[1])
    to_prev = pltpu.make_async_remote_copy(
        src_ref=p, dst_ref=r, send_sem=r_send.at[0], recv_sem=r_recv.at[0],
        device_id=(t - 1, sx, sy), device_id_type=MESH,
    )
    spread = [
        pltpu.make_async_remote_copy(
            src_ref=p, dst_ref=tot, send_sem=t_send.at[k], recv_sem=t_recv.at[0],
            device_id=(k, sx, sy), device_id_type=MESH,
        )
        for k in range(1, nt)
    ]

    @pl.when(not_last)
    def _():
        to_prev.wait_recv()
        p[...] += r[...]

    @pl.when(t > 0)
    def _():
        to_prev.start()
        spread[0].wait_recv()
        grad_ref[...] = tot[...]
        to_prev.wait_send()
        for copy in mains:
            copy.wait_send()

    @pl.when(t == 0)
    def _():
        for copy in spread:
            copy.start()
        grad_ref[...] = p[...]
        for copy in spread:
            copy.wait_send()

    for q, copy in first + second:
        wait_out(q[1], copy)
    for q, copy in around_m:
        wait_out(jnp.logical_and(last, q[1]), copy)
    for q, copy in down:
        wait_out(jnp.logical_and(t > 0, q[1]), copy)


def shards(sources, forward_states, terminal, damping, contact_stiff, regions):
    nt, ns = lax.axis_size("tm"), lax.axis_size("sx")
    steps, bx, by, cz = sources.shape
    assert steps == 2 and bx == BLOCK_CELLS and lax.axis_size("sy") == 2
    vmem = pl.BlockSpec(memory_space=pltpu.VMEM)
    hbm = pl.BlockSpec(memory_space=pltpu.HBM)
    f32 = jnp.float32
    ext = (bx + 2 * H, by + HY, cz)
    block = (bx, by, cz)
    dma = pltpu.SemaphoreType.DMA
    return pl.pallas_call(
        functools.partial(kernel, nt, ns),
        out_shape=(
            jax.ShapeDtypeStruct(sources.shape, f32),
            jax.ShapeDtypeStruct(block, f32),
        ),
        in_specs=[hbm] * 6,
        out_specs=(vmem, vmem),
        scratch_shapes=[
            pltpu.VMEM(sources.shape, f32),
            pltpu.VMEM(sources.shape, f32),
            pltpu.SMEM(contact_stiff.shape, f32),
            pltpu.SMEM(regions.shape, jnp.int32),
            pltpu.VMEM((6, 8, cz), f32),
            pltpu.VMEM((2,) + ext, f32),
            pltpu.VMEM((2,) + ext, f32),
            pltpu.VMEM(ext, f32),
            pltpu.VMEM(ext, f32),
            pltpu.VMEM(ext, f32),
            pltpu.VMEM(block, f32),
            pltpu.VMEM(block, f32),
            pltpu.VMEM(block, f32),
            pltpu.VMEM(block, f32),
            dma((6,)), dma((5,)), dma((5,)), dma((5,)), dma((5,)), dma((5,)),
            dma((9,)), dma((9,)), dma((1,)), dma((1,)), dma((nt,)), dma((1,)),
        ],
        compiler_params=pltpu.CompilerParams(
            collective_id=0, has_side_effects=True, vmem_limit_bytes=64 * 1024 * 1024
        ),
    )(sources, forward_states, terminal, damping, contact_stiff, regions)


def solution(mesh):
    in_specs = (
        P("tm", "sx", "sy", None),
        P("tm", "sx", "sy", None),
        P("sx", "sy", None),
        P("sx", "sy", None),
        P(),
        P("tm", "sx", "sy"),
    )
    out_specs = (P("tm", "sx", "sy", None), P("sx", "sy", None))
    return jax.shard_map(shards, mesh=mesh, in_specs=in_specs, out_specs=out_specs, check_vma=False)
```

```python
import functools

import jax
import jax.numpy as jnp
from jax import lax
from jax.experimental import pallas as pl
from jax.experimental.pallas import tpu as pltpu
from jax.sharding import PartitionSpec as P

MESH = pl.DeviceIdType.MESH
SWEEPS = 4
BLOCK_CELLS = 8
COUPLING = 0.5
H = SWEEPS
HY = 8

XLO, XHI, YS, CLO, CHI, MAIN0, MAIN1 = range(7)


def kernel(
    nt, ns, src_hbm, fs_hbm, term_hbm, damp_hbm, stiff_hbm, reg_hbm,
    adj_ref, grad_ref,
    src_ref, fs_ref, stiff_ref, reg_ref, picks, inv,
    g, m, xa, xb, c, r, p, tot,
    l_sem, g_send, g_recv, h_send, h_recv, u_send, m_send, m_recv, r_send, r_recv, t_send, t_recv,
):
    steps, bx, by, cz = src_ref.shape
    ex, ey = bx + 2 * H, by + HY
    parts = min(nt, bx)
    size = bx // parts
    t = lax.axis_index("tm")
    sx = lax.axis_index("sx")
    sy = lax.axis_index("sy")
    last = t == nt - 1
    other = 1 - sy
    has_lo, has_hi = sx > 0, sx < ns - 1
    always = t >= 0
    ys = pl.multiple_of(other * HY, HY)

    core = pl.ds(0, by)
    edge = pl.ds(ys, HY)
    far = pl.ds(by, HY)
    pieces = [
        (XHI, has_lo, sx - 1, sy, (0, H), H + bx, core, core),
        (XLO, has_hi, sx + 1, sy, (bx - H, bx), 0, core, core),
        (YS, always, sx, other, (0, bx), H, edge, far),
        (CHI, has_lo, sx - 1, other, (0, H - 1), H + bx, edge, far),
        (CLO, has_hi, sx + 1, other, (bx - H + 1, bx), 1, edge, far),
    ]
    arrives = {XLO: has_lo, XHI: has_hi, YS: always, CLO: has_lo, CHI: has_hi}

    body = pl.ds(H, bx)
    own = g.at[0, body, core]
    loads = [
        pltpu.make_async_copy(stiff_hbm, stiff_ref, l_sem.at[0]),
        pltpu.make_async_copy(reg_hbm, reg_ref, l_sem.at[1]),
        pltpu.make_async_copy(damp_hbm, g.at[1, body, core], l_sem.at[2]),
        pltpu.make_async_copy(src_hbm, src_ref, l_sem.at[3]),
        pltpu.make_async_copy(fs_hbm, fs_ref, l_sem.at[4]),
    ]
    from_term = pltpu.make_async_copy(term_hbm, own, l_sem.at[5])
    from_src = pltpu.make_async_copy(src_hbm.at[1], own, l_sem.at[5])
    for load in loads[:3]:
        load.start()

    @pl.when(t == nt - 1)
    def _():
        from_term.start()

    @pl.when(t != nt - 1)
    def _():
        from_src.start()

    for load in loads[3:]:
        load.start()

    edge_zero = jnp.zeros((H, ey, cz), jnp.float32)
    far_zero = jnp.zeros((bx, HY, cz), jnp.float32)
    for ref in (g.at[0], g.at[1], m):
        ref[0:H] = edge_zero
        ref[H + bx : ex] = edge_zero
        ref[H : H + bx, by:ey] = far_zero

    barrier = pltpu.get_barrier_semaphore()

    def greet(cond, dev):
        @pl.when(cond)
        def _():
            pl.semaphore_signal(barrier, inc=1, device_id=dev, device_id_type=MESH)

    for slot, cond, dx, dy, *_ in pieces:
        greet(cond, (t, dx, dy))
    for dt, cond_t in ((t - 1, t > 0), (t + 1, t < nt - 1)):
        for slot, cond, dx, dy, *_ in pieces:
            greet(jnp.logical_and(cond_t, cond), (dt, dx, dy))
    for k in range(nt):
        greet(t != k, (k, sx, sy))
    one = lambda cond: jnp.where(cond, 1, 0)
    around = 2 * (one(has_lo) + one(has_hi)) + 1
    slabs = one(t > 0) + one(t < nt - 1)
    friends = around + slabs * around + nt - 1

    blocks = by // BLOCK_CELLS
    for load in loads[:2]:
        load.wait()
    late = jnp.where(t == nt - 1, 1, 0)
    for j in range(blocks):
        for k, step in enumerate((late, 1 - late)):
            value = stiff_ref[reg_ref[step, 0, j]]
            picks[5, j * steps + k : j * steps + k + 1, :] = jnp.full((1, cz), value, jnp.float32)

    def piece_copy(piece, src, off, dst, dt, send, recv, fields=None):
        slot, cond, dx, dy, (lo, hi), to, ysrc, ydst = piece
        s_at = (pl.ds(off + lo, hi - lo), ysrc)
        d_at = (pl.ds(to, hi - lo), ydst)
        if fields is not None:
            s_at, d_at = (fields,) + s_at, (fields,) + d_at
        return pltpu.make_async_remote_copy(
            src_ref=src.at[s_at], dst_ref=dst.at[d_at],
            send_sem=send.at[slot], recv_sem=recv.at[slot],
            device_id=(dt, dx, dy), device_id_type=MESH,
        )

    def start(cond, copy):
        @pl.when(cond)
        def _():
            copy.start()

    def wait_in(cond, copy):
        @pl.when(cond)
        def _():
            copy.wait_recv()

    def wait_out(cond, copy):
        @pl.when(cond)
        def _():
            copy.wait_send()

    first = [(q, piece_copy(q, g, H, g, t, g_send, g_recv, pl.ds(0, 2))) for q in pieces]
    second = [
        (
            q,
            pltpu.make_async_remote_copy(
                src_ref=picks.at[5], dst_ref=picks.at[q[0]],
                send_sem=h_send.at[q[0]], recv_sem=h_recv.at[q[0]],
                device_id=(t, q[2], q[3]), device_id_type=MESH,
            ),
        )
        for q in pieces
    ]
    around_m = [(q, piece_copy(q, m, H, m, t, u_send, m_recv)) for q in pieces]
    down = [(q, piece_copy(q, c, 0, m, t - 1, m_send, m_recv)) for q in pieces]
    chunks = 4
    half = bx // chunks
    mains = [
        pltpu.make_async_remote_copy(
            src_ref=c.at[pl.ds(i * half, half)], dst_ref=m.at[pl.ds(H + i * half, half), core],
            send_sem=m_send.at[MAIN0 + i], recv_sem=m_recv.at[MAIN0 + i],
            device_id=(t - 1, sx, sy), device_id_type=MESH,
        )
        for i in range(chunks)
    ]

    pl.semaphore_wait(barrier, friends)
    for q, copy in second:
        start(q[1], copy)
    loads[2].wait()
    from_src.wait()
    for q, copy in first:
        start(q[1], copy)

    lane = lax.broadcasted_iota(jnp.int32, (ey, cz), 1)
    row = lax.broadcasted_iota(jnp.int32, (ey, cz), 0)
    no_before = jnp.logical_and(row == 0, sy == 0)
    no_after = jnp.logical_and(row == by - 1, sy == 1)
    z_first, z_last = lane == 0, lane == cz - 1

    def phi(b, inv):
        bufs = [b, xa, xb]
        cur = b
        out = []
        for s in range(1, SWEEPS + 1):
            nxt = xa if s % 2 else xb
            for i in range(s, ex - s):
                x = cur[i]
                total = cur[i - 1] + cur[i + 1]
                total += jnp.where(no_before, 0.0, pltpu.roll(x, 1, 0))
                total += jnp.where(no_after, 0.0, pltpu.roll(x, ey - 1, 0))
                total += jnp.where(z_first, 0.0, pltpu.roll(x, 1, 1))
                total += jnp.where(z_last, 0.0, pltpu.roll(x, cz - 1, 1))
                value = (b[i] + COUPLING * total) * inv[i]
                if s == SWEEPS:
                    out.append(value[:by])
                else:
                    nxt[i] = value
            cur = nxt
        return out

    def arrived(copies):
        for q, copy in copies:
            wait_in(arrives[q[0]], copy)

    def pick(slot, j, k):
        return picks[slot, j * steps + k : j * steps + k + 1, :]

    def near_pick(slot, k):
        if blocks == 1:
            return pick(slot, 0, k)
        return jnp.where(sy == 1, pick(slot, blocks - 1, k), pick(slot, 0, k))

    def fill(out, k, rows, straight, corner, inside):
        for i in rows:
            for j in range(blocks):
                cells = slice(j * BLOCK_CELLS, (j + 1) * BLOCK_CELLS)
                value = 1.0 / (1.0 + (pick(straight, j, k) + g[1, i, cells, :]) + 6.0 * COUPLING)
                inv[out, i, cells, :] = jnp.where(inside, value, 0.0)
            value = 1.0 / (1.0 + (near_pick(corner, k) + g[1, i, by:ey, :]) + 6.0 * COUPLING)
            inv[out, i, by:ey, :] = jnp.where(inside, value, 0.0)

    def fill_all(out, k):
        fill(out, k, range(1, H), XLO, CLO, has_lo)
        fill(out, k, range(H, H + bx), 5, YS, always)
        fill(out, k, range(H + bx, ex - 1), XHI, CHI, has_hi)

    loads[3].wait()
    arrived(second)
    arrived(first)
    fill_all(0, 0)
    y1 = phi(g.at[0], inv.at[0])

    @pl.when(last)
    def _():
        for i in range(bx):
            value = y1[i] + src_ref[1, i]
            adj_ref[1, i] = value
            m[H + i, core, :] = value
        for q, copy in around_m:
            start(q[1], copy)

    fill_all(1, 1)

    @pl.when(last)
    def _():
        arrived(around_m)
        top = phi(m, inv.at[1])
        for i in range(bx):
            c[i] = top[i] + src_ref[0, i]

    not_last = jnp.logical_not(last)

    @pl.when(not_last)
    def _():
        for j in range(blocks):
            cells = slice(j * BLOCK_CELLS, (j + 1) * BLOCK_CELLS)
            c[:, cells, :] = 1.0 / (1.0 + steps * (pick(5, j, 0) + g[1, H : H + bx, cells, :]))
        for i in range(bx):
            adj_ref[0, i] = y1[i] + src_ref[0, i]

    for i in range(chunks):
        rows = pl.ds(i * half, half)

        @pl.when(not_last)
        def _():
            mains[i].wait_recv()
            c[rows] = c[rows] * m[pl.ds(H + i * half, half), core, :] + adj_ref[0, rows]

        start(t > 0, mains[i])
    for q, copy in down:
        start(jnp.logical_and(t > 0, q[1]), copy)
    adj_ref[0] = c[...]

    @pl.when(not_last)
    def _():
        arrived(down)
        top = phi(m, inv.at[1])
        for i in range(bx):
            adj_ref[1, i] = top[i] + src_ref[1, i]

    loads[4].wait()
    p[...] = -(adj_ref[0] * fs_ref[0] + adj_ref[1] * fs_ref[1])

    def part(q):
        return pl.ds(q * size, size)

    def gather_copy(q):
        return pltpu.make_async_remote_copy(
            src_ref=p.at[part(q)], dst_ref=r.at[t], send_sem=r_send.at[q], recv_sem=r_recv.at[t],
            device_id=(q, sx, sy), device_id_type=MESH,
        )

    def arrival(k):
        return pltpu.make_async_remote_copy(
            src_ref=p.at[part(0)], dst_ref=r.at[k], send_sem=r_send.at[0], recv_sem=r_recv.at[k],
            device_id=(0, sx, sy), device_id_type=MESH,
        )

    def spread_copy(q, k):
        return pltpu.make_async_remote_copy(
            src_ref=tot.at[part(q)], dst_ref=tot.at[part(q)], send_sem=t_send.at[k],
            recv_sem=t_recv.at[q], device_id=(k, sx, sy), device_id_type=MESH,
        )

    for q in range(parts):
        start(t != q, gather_copy(q))
    for q in range(parts):

        @pl.when(t == q)
        def _():
            total = p[part(q)]
            for k in range(nt):
                if k != q:
                    arrival(k).wait_recv()
                    total += r[k]
            tot[part(q)] = total
            for k in range(nt):
                if k != q:
                    spread_copy(q, k).start()

    for q in range(parts):
        wait_in(t != q, spread_copy(q, 0))
    grad_ref[...] = tot[...]
    for q in range(parts):
        wait_out(t != q, gather_copy(q))

        @pl.when(t == q)
        def _():
            for k in range(nt):
                if k != q:
                    spread_copy(q, k).wait_send()

    @pl.when(t > 0)
    def _():
        for copy in mains:
            copy.wait_send()

    for q, copy in first + second:
        wait_out(q[1], copy)
    for q, copy in around_m:
        wait_out(jnp.logical_and(last, q[1]), copy)
    for q, copy in down:
        wait_out(jnp.logical_and(t > 0, q[1]), copy)


def shards(sources, forward_states, terminal, damping, contact_stiff, regions):
    nt, ns = lax.axis_size("tm"), lax.axis_size("sx")
    steps, bx, by, cz = sources.shape
    assert steps == 2 and bx == BLOCK_CELLS and lax.axis_size("sy") == 2
    vmem = pl.BlockSpec(memory_space=pltpu.VMEM)
    hbm = pl.BlockSpec(memory_space=pltpu.HBM)
    f32 = jnp.float32
    ext = (bx + 2 * H, by + HY, cz)
    block = (bx, by, cz)
    dma = pltpu.SemaphoreType.DMA
    return pl.pallas_call(
        functools.partial(kernel, nt, ns),
        out_shape=(
            jax.ShapeDtypeStruct(sources.shape, f32),
            jax.ShapeDtypeStruct(block, f32),
        ),
        in_specs=[hbm] * 6,
        out_specs=(vmem, vmem),
        scratch_shapes=[
            pltpu.VMEM(sources.shape, f32),
            pltpu.VMEM(sources.shape, f32),
            pltpu.SMEM(contact_stiff.shape, f32),
            pltpu.SMEM(regions.shape, jnp.int32),
            pltpu.VMEM((6, 8, cz), f32),
            pltpu.VMEM((2,) + ext, f32),
            pltpu.VMEM((2,) + ext, f32),
            pltpu.VMEM(ext, f32),
            pltpu.VMEM(ext, f32),
            pltpu.VMEM(ext, f32),
            pltpu.VMEM(block, f32),
            pltpu.VMEM((nt, bx // min(nt, bx), by, cz), f32),
            pltpu.VMEM(block, f32),
            pltpu.VMEM(block, f32),
            dma((6,)), dma((5,)), dma((5,)), dma((5,)), dma((5,)), dma((5,)),
            dma((9,)), dma((9,)), dma((nt,)), dma((nt,)), dma((nt,)), dma((nt,)),
        ],
        compiler_params=pltpu.CompilerParams(
            collective_id=0, has_side_effects=True, vmem_limit_bytes=64 * 1024 * 1024
        ),
    )(sources, forward_states, terminal, damping, contact_stiff, regions)


def solution(mesh):
    in_specs = (
        P("tm", "sx", "sy", None),
        P("tm", "sx", "sy", None),
        P("sx", "sy", None),
        P("sx", "sy", None),
        P(),
        P("tm", "sx", "sy"),
    )
    out_specs = (P("tm", "sx", "sy", None), P("sx", "sy", None))
    return jax.shard_map(shards, mesh=mesh, in_specs=in_specs, out_specs=out_specs, check_vma=False)
```

```python
import functools

import jax
import jax.numpy as jnp
from jax import lax
from jax.experimental import pallas as pl
from jax.experimental.pallas import tpu as pltpu
from jax.sharding import PartitionSpec as P

MESH = pl.DeviceIdType.MESH
SWEEPS = 4
BLOCK_CELLS = 8
COUPLING = 0.5
H = SWEEPS
HY = 8

XLO, XHI, YS, CLO, CHI, MAIN0, MAIN1 = range(7)


def kernel(
    nt, ns, src_hbm, fs_hbm, term_hbm, damp_hbm, stiff_hbm, reg_hbm,
    adj_hbm, grad_hbm,
    adj_ref, grad_ref, src_ref, fs_ref, stiff_ref, reg_ref, picks, inv,
    g, m, xa, xb, c, r, p, tot,
    l_sem, o_sem, g_send, g_recv, h_send, h_recv, u_send, m_send, m_recv, r_send, r_recv, t_send, t_recv,
):
    steps, bx, by, cz = src_ref.shape
    ex, ey = bx + 2 * H, by + HY
    t = lax.axis_index("tm")
    sx = lax.axis_index("sx")
    sy = lax.axis_index("sy")
    last = t == nt - 1
    other = 1 - sy
    has_lo, has_hi = sx > 0, sx < ns - 1
    always = t >= 0
    ys = pl.multiple_of(other * HY, HY)

    core = pl.ds(0, by)
    edge = pl.ds(ys, HY)
    far = pl.ds(by, HY)
    pieces = [
        (XHI, has_lo, sx - 1, sy, (0, H), H + bx, core, core),
        (XLO, has_hi, sx + 1, sy, (bx - H, bx), 0, core, core),
        (YS, always, sx, other, (0, bx), H, edge, far),
        (CHI, has_lo, sx - 1, other, (0, H - 1), H + bx, edge, far),
        (CLO, has_hi, sx + 1, other, (bx - H + 1, bx), 1, edge, far),
    ]
    arrives = {XLO: has_lo, XHI: has_hi, YS: always, CLO: has_lo, CHI: has_hi}

    body = pl.ds(H, bx)
    own = g.at[0, body, core]
    loads = [
        pltpu.make_async_copy(stiff_hbm, stiff_ref, l_sem.at[0]),
        pltpu.make_async_copy(reg_hbm, reg_ref, l_sem.at[1]),
        pltpu.make_async_copy(damp_hbm, g.at[1, body, core], l_sem.at[2]),
        pltpu.make_async_copy(src_hbm, src_ref, l_sem.at[3]),
        pltpu.make_async_copy(fs_hbm, fs_ref, l_sem.at[4]),
    ]
    from_term = pltpu.make_async_copy(term_hbm, own, l_sem.at[5])
    from_src = pltpu.make_async_copy(src_hbm.at[1], own, l_sem.at[5])
    for load in loads[:3]:
        load.start()

    @pl.when(t == nt - 1)
    def _():
        from_term.start()

    @pl.when(t != nt - 1)
    def _():
        from_src.start()

    for load in loads[3:]:
        load.start()

    edge_zero = jnp.zeros((H, ey, cz), jnp.float32)
    far_zero = jnp.zeros((bx, HY, cz), jnp.float32)
    for ref in (g.at[0], g.at[1], m):
        ref[0:H] = edge_zero
        ref[H + bx : ex] = edge_zero
        ref[H : H + bx, by:ey] = far_zero

    barrier = pltpu.get_barrier_semaphore()

    def greet(cond, dev):
        @pl.when(cond)
        def _():
            pl.semaphore_signal(barrier, inc=1, device_id=dev, device_id_type=MESH)

    for slot, cond, dx, dy, *_ in pieces:
        greet(cond, (t, dx, dy))
    for dt, cond_t in ((t - 1, t > 0), (t + 1, t < nt - 1)):
        greet(cond_t, (dt, sx, sy))
        for slot, cond, dx, dy, *_ in pieces:
            greet(jnp.logical_and(cond_t, cond), (dt, dx, dy))
    for owner in range(2):
        greet(t > owner + 1, (owner, sx, sy))
        for k in range(owner + 2, nt):
            greet(t == owner, (k, sx, sy))
    one = lambda cond: jnp.where(cond, 1, 0)
    around = 2 * (one(has_lo) + one(has_hi)) + 1
    slabs = one(t > 0) + one(t < nt - 1)
    friends = around + slabs * (around + 1) + one(t > 1) + one(t > 2)
    friends += one(t == 0) * (nt - 2) + one(t == 1) * (nt - 3)

    blocks = by // BLOCK_CELLS
    for load in loads[:2]:
        load.wait()
    late = jnp.where(t == nt - 1, 1, 0)
    for j in range(blocks):
        for k, step in enumerate((late, 1 - late)):
            value = stiff_ref[reg_ref[step, 0, j]]
            picks[5, j * steps + k : j * steps + k + 1, :] = jnp.full((1, cz), value, jnp.float32)

    def piece_copy(piece, src, off, dst, dt, send, recv, fields=None):
        slot, cond, dx, dy, (lo, hi), to, ysrc, ydst = piece
        s_at = (pl.ds(off + lo, hi - lo), ysrc)
        d_at = (pl.ds(to, hi - lo), ydst)
        if fields is not None:
            s_at, d_at = (fields,) + s_at, (fields,) + d_at
        return pltpu.make_async_remote_copy(
            src_ref=src.at[s_at], dst_ref=dst.at[d_at],
            send_sem=send.at[slot], recv_sem=recv.at[slot],
            device_id=(dt, dx, dy), device_id_type=MESH,
        )

    def start(cond, copy):
        @pl.when(cond)
        def _():
            copy.start()

    def wait_in(cond, copy):
        @pl.when(cond)
        def _():
            copy.wait_recv()

    def wait_out(cond, copy):
        @pl.when(cond)
        def _():
            copy.wait_send()

    first = [(q, piece_copy(q, g, H, g, t, g_send, g_recv, pl.ds(0, 2))) for q in pieces]
    second = [
        (
            q,
            pltpu.make_async_remote_copy(
                src_ref=picks.at[5], dst_ref=picks.at[q[0]],
                send_sem=h_send.at[q[0]], recv_sem=h_recv.at[q[0]],
                device_id=(t, q[2], q[3]), device_id_type=MESH,
            ),
        )
        for q in pieces
    ]
    around_m = [(q, piece_copy(q, m, H, m, t, u_send, m_recv)) for q in pieces]
    down = [(q, piece_copy(q, c, 0, m, t - 1, m_send, m_recv)) for q in pieces]
    chunks = 4
    half = bx // chunks
    mains = [
        pltpu.make_async_remote_copy(
            src_ref=c.at[pl.ds(i * half, half)], dst_ref=m.at[pl.ds(H + i * half, half), core],
            send_sem=m_send.at[MAIN0 + i], recv_sem=m_recv.at[MAIN0 + i],
            device_id=(t - 1, sx, sy), device_id_type=MESH,
        )
        for i in range(chunks)
    ]

    pl.semaphore_wait(barrier, friends)
    for q, copy in second:
        start(q[1], copy)
    loads[2].wait()
    from_src.wait()
    for q, copy in first:
        start(q[1], copy)

    lane = lax.broadcasted_iota(jnp.int32, (ey, cz), 1)
    row = lax.broadcasted_iota(jnp.int32, (ey, cz), 0)
    no_before = jnp.logical_and(row == 0, sy == 0)
    no_after = jnp.logical_and(row == by - 1, sy == 1)
    z_first, z_last = lane == 0, lane == cz - 1

    def phi(b, inv):
        bufs = [b, xa, xb]
        cur = b
        out = []
        for s in range(1, SWEEPS + 1):
            nxt = xa if s % 2 else xb
            for i in range(s, ex - s):
                x = cur[i]
                total = cur[i - 1] + cur[i + 1]
                total += jnp.where(no_before, 0.0, pltpu.roll(x, 1, 0))
                total += jnp.where(no_after, 0.0, pltpu.roll(x, ey - 1, 0))
                total += jnp.where(z_first, 0.0, pltpu.roll(x, 1, 1))
                total += jnp.where(z_last, 0.0, pltpu.roll(x, cz - 1, 1))
                value = (b[i] + COUPLING * total) * inv[i]
                if s == SWEEPS:
                    out.append(value[:by])
                else:
                    nxt[i] = value
            cur = nxt
        return out

    def arrived(copies):
        for q, copy in copies:
            wait_in(arrives[q[0]], copy)

    def pick(slot, j, k):
        return picks[slot, j * steps + k : j * steps + k + 1, :]

    def near_pick(slot, k):
        if blocks == 1:
            return pick(slot, 0, k)
        return jnp.where(sy == 1, pick(slot, blocks - 1, k), pick(slot, 0, k))

    def fill(out, k, rows, straight, corner, inside):
        for i in rows:
            for j in range(blocks):
                cells = slice(j * BLOCK_CELLS, (j + 1) * BLOCK_CELLS)
                value = 1.0 / (1.0 + (pick(straight, j, k) + g[1, i, cells, :]) + 6.0 * COUPLING)
                inv[out, i, cells, :] = jnp.where(inside, value, 0.0)
            value = 1.0 / (1.0 + (near_pick(corner, k) + g[1, i, by:ey, :]) + 6.0 * COUPLING)
            inv[out, i, by:ey, :] = jnp.where(inside, value, 0.0)

    def fill_all(out, k):
        fill(out, k, range(1, H), XLO, CLO, has_lo)
        fill(out, k, range(H, H + bx), 5, YS, always)
        fill(out, k, range(H + bx, ex - 1), XHI, CHI, has_hi)

    loads[3].wait()
    arrived(second)
    arrived(first)
    fill_all(0, 0)
    y1 = phi(g.at[0], inv.at[0])

    @pl.when(last)
    def _():
        for i in range(bx):
            value = y1[i] + src_ref[1, i]
            adj_ref[1, i] = value
            m[H + i, core, :] = value
        for q, copy in around_m:
            start(q[1], copy)

    fill_all(1, 1)

    @pl.when(last)
    def _():
        arrived(around_m)
        top = phi(m, inv.at[1])
        for i in range(bx):
            c[i] = top[i] + src_ref[0, i]

    not_last = jnp.logical_not(last)

    @pl.when(not_last)
    def _():
        for j in range(blocks):
            cells = slice(j * BLOCK_CELLS, (j + 1) * BLOCK_CELLS)
            c[:, cells, :] = 1.0 / (1.0 + steps * (pick(5, j, 0) + g[1, H : H + bx, cells, :]))
        for i in range(bx):
            adj_ref[0, i] = y1[i] + src_ref[0, i]

    for i in range(chunks):
        rows = pl.ds(i * half, half)

        @pl.when(not_last)
        def _():
            mains[i].wait_recv()
            c[rows] = c[rows] * m[pl.ds(H + i * half, half), core, :] + adj_ref[0, rows]

        start(t > 0, mains[i])
    for q, copy in down:
        start(jnp.logical_and(t > 0, q[1]), copy)
    adj_ref[0] = c[...]
    saves = [
        pltpu.make_async_copy(adj_ref.at[k], adj_hbm.at[k], o_sem.at[k]) for k in range(steps)
    ]
    saves[0].start()
    loads[4].wait()
    p[...] = c[...] * fs_ref[0]

    @pl.when(not_last)
    def _():
        arrived(down)
        top = phi(m, inv.at[1])
        for i in range(bx):
            adj_ref[1, i] = top[i] + src_ref[1, i]

    p[...] = -(p[...] + adj_ref[1] * fs_ref[1])
    to_prev = pltpu.make_async_remote_copy(
        src_ref=p, dst_ref=r, send_sem=r_send.at[0], recv_sem=r_recv.at[0],
        device_id=(t - 1, sx, sy), device_id_type=MESH,
    )

    def spread(owner, k):
        return pltpu.make_async_remote_copy(
            src_ref=p, dst_ref=tot.at[owner], send_sem=t_send.at[k], recv_sem=t_recv.at[owner],
            device_id=(k, sx, sy), device_id_type=MESH,
        )

    @pl.when(jnp.logical_and(not_last, t > 0))
    def _():
        to_prev.wait_recv()
        p[...] += r[...]

    @pl.when(t >= 2)
    def _():
        to_prev.start()

    for owner in range(2):

        @pl.when(t == owner)
        def _():
            for k in range(nt - 1, -1, -1):
                if k != owner:
                    spread(owner, k).start()
            tot[owner] = p[...]

    saves[1].start()
    for owner in range(2):
        wait_in(t != owner, spread(owner, 0))
    grad_ref[...] = tot[0] + tot[1]
    save_grad = pltpu.make_async_copy(grad_ref, grad_hbm, o_sem.at[2])
    save_grad.start()

    @pl.when(t >= 2)
    def _():
        to_prev.wait_send()

    for owner in range(2):

        @pl.when(t == owner)
        def _():
            for k in range(nt):
                if k != owner:
                    spread(owner, k).wait_send()

    @pl.when(t > 0)
    def _():
        for copy in mains:
            copy.wait_send()

    for q, copy in first + second:
        wait_out(q[1], copy)
    for q, copy in around_m:
        wait_out(jnp.logical_and(last, q[1]), copy)
    for q, copy in down:
        wait_out(jnp.logical_and(t > 0, q[1]), copy)
    for save in saves:
        save.wait()
    save_grad.wait()


def shards(sources, forward_states, terminal, damping, contact_stiff, regions):
    nt, ns = lax.axis_size("tm"), lax.axis_size("sx")
    steps, bx, by, cz = sources.shape
    assert nt > 2 and steps == 2 and bx == BLOCK_CELLS and lax.axis_size("sy") == 2
    hbm = pl.BlockSpec(memory_space=pltpu.HBM)
    f32 = jnp.float32
    ext = (bx + 2 * H, by + HY, cz)
    block = (bx, by, cz)
    dma = pltpu.SemaphoreType.DMA
    return pl.pallas_call(
        functools.partial(kernel, nt, ns),
        out_shape=(
            jax.ShapeDtypeStruct(sources.shape, f32),
            jax.ShapeDtypeStruct(block, f32),
        ),
        in_specs=[hbm] * 6,
        out_specs=(hbm, hbm),
        scratch_shapes=[
            pltpu.VMEM(sources.shape, f32),
            pltpu.VMEM(block, f32),
            pltpu.VMEM(sources.shape, f32),
            pltpu.VMEM(sources.shape, f32),
            pltpu.SMEM(contact_stiff.shape, f32),
            pltpu.SMEM(regions.shape, jnp.int32),
            pltpu.VMEM((6, 8, cz), f32),
            pltpu.VMEM((2,) + ext, f32),
            pltpu.VMEM((2,) + ext, f32),
            pltpu.VMEM(ext, f32),
            pltpu.VMEM(ext, f32),
            pltpu.VMEM(ext, f32),
            pltpu.VMEM(block, f32),
            pltpu.VMEM(block, f32),
            pltpu.VMEM(block, f32),
            pltpu.VMEM((2,) + block, f32),
            dma((6,)), dma((3,)), dma((5,)), dma((5,)), dma((5,)), dma((5,)), dma((5,)),
            dma((9,)), dma((9,)), dma((1,)), dma((1,)), dma((nt,)), dma((2,)),
        ],
        compiler_params=pltpu.CompilerParams(
            collective_id=0, has_side_effects=True, vmem_limit_bytes=64 * 1024 * 1024
        ),
    )(sources, forward_states, terminal, damping, contact_stiff, regions)


def solution(mesh):
    in_specs = (
        P("tm", "sx", "sy", None),
        P("tm", "sx", "sy", None),
        P("sx", "sy", None),
        P("sx", "sy", None),
        P(),
        P("tm", "sx", "sy"),
    )
    out_specs = (P("tm", "sx", "sy", None), P("sx", "sy", None))
    return jax.shard_map(shards, mesh=mesh, in_specs=in_specs, out_specs=out_specs, check_vma=False)
```

```python
import functools

import jax
import jax.numpy as jnp
from jax import lax
from jax.experimental import pallas as pl
from jax.experimental.pallas import tpu as pltpu
from jax.sharding import PartitionSpec as P

MESH = pl.DeviceIdType.MESH
SWEEPS = 4
BLOCK_CELLS = 8
COUPLING = 0.5
H = SWEEPS
HY = 8

XLO, XHI, YS, CLO, CHI, MAIN0, MAIN1 = range(7)


def kernel(
    nt, ns, src_hbm, fs_hbm, term_hbm, damp_hbm, stiff_hbm, reg_hbm,
    adj_hbm, grad_hbm,
    adj_ref, grad_ref, src_ref, fs_ref, stiff_ref, reg_ref, picks, inv,
    g, m, xa, xb, c, r, p, tot,
    l_sem, o_sem, d_send, d_recv, g_send, g_recv, h_send, h_recv, u_send, m_send, m_recv, r_send, r_recv, t_send, t_recv,
):
    steps, bx, by, cz = src_ref.shape
    ex, ey = bx + 2 * H, by + HY
    t = lax.axis_index("tm")
    sx = lax.axis_index("sx")
    sy = lax.axis_index("sy")
    last = t == nt - 1
    other = 1 - sy
    has_lo, has_hi = sx > 0, sx < ns - 1
    always = t >= 0
    ys = pl.multiple_of(other * HY, HY)

    core = pl.ds(0, by)
    edge = pl.ds(ys, HY)
    far = pl.ds(by, HY)
    pieces = [
        (XHI, has_lo, sx - 1, sy, (0, H), H + bx, core, core),
        (XLO, has_hi, sx + 1, sy, (bx - H, bx), 0, core, core),
        (YS, always, sx, other, (0, bx), H, edge, far),
        (CHI, has_lo, sx - 1, other, (0, H - 1), H + bx, edge, far),
        (CLO, has_hi, sx + 1, other, (bx - H + 1, bx), 1, edge, far),
    ]
    arrives = {XLO: has_lo, XHI: has_hi, YS: always, CLO: has_lo, CHI: has_hi}

    body = pl.ds(H, bx)
    own = g.at[0, body, core]
    loads = [
        pltpu.make_async_copy(stiff_hbm, stiff_ref, l_sem.at[0]),
        pltpu.make_async_copy(reg_hbm, reg_ref, l_sem.at[1]),
        pltpu.make_async_copy(damp_hbm, g.at[1, body, core], l_sem.at[2]),
        pltpu.make_async_copy(src_hbm, src_ref, l_sem.at[3]),
        pltpu.make_async_copy(fs_hbm, fs_ref, l_sem.at[4]),
    ]
    from_term = pltpu.make_async_copy(term_hbm, own, l_sem.at[5])
    from_src = pltpu.make_async_copy(src_hbm.at[1], own, l_sem.at[5])
    for load in loads[:3]:
        load.start()

    @pl.when(t == nt - 1)
    def _():
        from_term.start()

    @pl.when(t != nt - 1)
    def _():
        from_src.start()

    for load in loads[3:]:
        load.start()

    edge_zero = jnp.zeros((H, ey, cz), jnp.float32)
    far_zero = jnp.zeros((bx, HY, cz), jnp.float32)
    for ref in (g.at[0], g.at[1], m):
        ref[0:H] = edge_zero
        ref[H + bx : ex] = edge_zero
        ref[H : H + bx, by:ey] = far_zero

    barrier = pltpu.get_barrier_semaphore()

    def greet(cond, dev):
        @pl.when(cond)
        def _():
            pl.semaphore_signal(barrier, inc=1, device_id=dev, device_id_type=MESH)

    for slot, cond, dx, dy, *_ in pieces:
        greet(cond, (t, dx, dy))
    for dt, cond_t in ((t - 1, t > 0), (t + 1, t < nt - 1)):
        greet(cond_t, (dt, sx, sy))
        for slot, cond, dx, dy, *_ in pieces:
            greet(jnp.logical_and(cond_t, cond), (dt, dx, dy))
    for owner in range(2):
        greet(t > owner + 1, (owner, sx, sy))
        for k in range(owner + 2, nt):
            greet(t == owner, (k, sx, sy))
    one = lambda cond: jnp.where(cond, 1, 0)
    around = 2 * (one(has_lo) + one(has_hi)) + 1
    slabs = one(t > 0) + one(t < nt - 1)
    friends = around + slabs * (around + 1) + one(t > 1) + one(t > 2)
    friends += one(t == 0) * (nt - 2) + one(t == 1) * (nt - 3)

    blocks = by // BLOCK_CELLS
    for load in loads[:2]:
        load.wait()
    late = jnp.where(last, 1, 0)
    for j in range(blocks):
        for k, step in enumerate((late, 1 - late)):
            value = stiff_ref[reg_ref[step, 0, j]]
            picks[5, j * steps + k : j * steps + k + 1, :] = jnp.full((1, cz), value, jnp.float32)

    def piece_copy(piece, src, off, dst, dt, send, recv, fields=None):
        slot, cond, dx, dy, (lo, hi), to, ysrc, ydst = piece
        s_at = (pl.ds(off + lo, hi - lo), ysrc)
        d_at = (pl.ds(to, hi - lo), ydst)
        if fields is not None:
            s_at, d_at = (fields,) + s_at, (fields,) + d_at
        return pltpu.make_async_remote_copy(
            src_ref=src.at[s_at], dst_ref=dst.at[d_at],
            send_sem=send.at[slot], recv_sem=recv.at[slot],
            device_id=(dt, dx, dy), device_id_type=MESH,
        )

    def start(cond, copy):
        @pl.when(cond)
        def _():
            copy.start()

    def wait_in(cond, copy):
        @pl.when(cond)
        def _():
            copy.wait_recv()

    def wait_out(cond, copy):
        @pl.when(cond)
        def _():
            copy.wait_send()

    first = [(q, piece_copy(q, g, H, g, t, g_send, g_recv, pl.ds(0, 2))) for q in pieces]
    alone = [(q, piece_copy(q, g, H, g, t, g_send, g_recv, pl.ds(0, 1))) for q in pieces]
    up = [(q, piece_copy(q, g, H, g, t + 1, d_send, d_recv, pl.ds(1, 1))) for q in pieces]
    second = [
        (
            q,
            pltpu.make_async_remote_copy(
                src_ref=picks.at[5], dst_ref=picks.at[q[0]],
                send_sem=h_send.at[q[0]], recv_sem=h_recv.at[q[0]],
                device_id=(t, q[2], q[3]), device_id_type=MESH,
            ),
        )
        for q in pieces
    ]
    around_m = [(q, piece_copy(q, m, H, m, t, u_send, m_recv)) for q in pieces]
    down = [(q, piece_copy(q, c, 0, m, t - 1, m_send, m_recv)) for q in pieces]
    chunks = 4
    half = bx // chunks
    mains = [
        pltpu.make_async_remote_copy(
            src_ref=c.at[pl.ds(i * half, half)], dst_ref=m.at[pl.ds(H + i * half, half), core],
            send_sem=m_send.at[MAIN0 + i], recv_sem=m_recv.at[MAIN0 + i],
            device_id=(t - 1, sx, sy), device_id_type=MESH,
        )
        for i in range(chunks)
    ]

    pl.semaphore_wait(barrier, friends)
    loads[2].wait()

    @pl.when(t == nt - 2)
    def _():
        for q, copy in up:
            start(q[1], copy)

    from_src.wait()

    @pl.when(last)
    def _():
        for q, copy in alone:
            start(q[1], copy)

    @pl.when(jnp.logical_not(last))
    def _():
        for q, copy in first:
            start(q[1], copy)

    for q, copy in second:
        start(q[1], copy)

    lane = lax.broadcasted_iota(jnp.int32, (ey, cz), 1)
    row = lax.broadcasted_iota(jnp.int32, (ey, cz), 0)
    no_before = jnp.logical_and(row == 0, sy == 0)
    no_after = jnp.logical_and(row == by - 1, sy == 1)
    z_first, z_last = lane == 0, lane == cz - 1

    def phi(b, inv):
        bufs = [b, xa, xb]
        cur = b
        out = []
        for s in range(1, SWEEPS + 1):
            nxt = xa if s % 2 else xb
            for i in range(s, ex - s):
                x = cur[i]
                total = cur[i - 1] + cur[i + 1]
                total += jnp.where(no_before, 0.0, pltpu.roll(x, 1, 0))
                total += jnp.where(no_after, 0.0, pltpu.roll(x, ey - 1, 0))
                total += jnp.where(z_first, 0.0, pltpu.roll(x, 1, 1))
                total += jnp.where(z_last, 0.0, pltpu.roll(x, cz - 1, 1))
                value = (b[i] + COUPLING * total) * inv[i]
                if s == SWEEPS:
                    out.append(value[:by])
                else:
                    nxt[i] = value
            cur = nxt
        return out

    def arrived(copies):
        for q, copy in copies:
            wait_in(arrives[q[0]], copy)

    def pick(slot, j, k):
        return picks[slot, j * steps + k : j * steps + k + 1, :]

    def near_pick(slot, k):
        if blocks == 1:
            return pick(slot, 0, k)
        return jnp.where(sy == 1, pick(slot, blocks - 1, k), pick(slot, 0, k))

    def inverse(at, i, cells):
        return 1.0 / (1.0 + (at + g[1, i, cells, :]) + 6.0 * COUPLING)

    def fill_own(out):
        for i in range(H, H + bx):
            for j in range(blocks):
                cells = slice(j * BLOCK_CELLS, (j + 1) * BLOCK_CELLS)
                inv[out, i, cells, :] = inverse(pick(5, j, out), i, cells)

    def fill_halo(out):
        for rows, straight, corner, inside in (
            (range(1, H), XLO, CLO, has_lo),
            (range(H + bx, ex - 1), XHI, CHI, has_hi),
        ):
            for i in rows:
                for j in range(blocks):
                    cells = slice(j * BLOCK_CELLS, (j + 1) * BLOCK_CELLS)
                    value = inverse(pick(straight, j, out), i, cells)
                    inv[out, i, cells, :] = jnp.where(inside, value, 0.0)
                value = inverse(near_pick(corner, out), i, slice(by, ey))
                inv[out, i, by:ey, :] = jnp.where(inside, value, 0.0)
        for i in range(H, H + bx):
            inv[out, i, by:ey, :] = inverse(near_pick(YS, out), i, slice(by, ey))

    fill_own(0)
    fill_own(1)
    loads[3].wait()
    arrived(second)

    @pl.when(last)
    def _():
        arrived(up)
        arrived(alone)

    @pl.when(jnp.logical_not(last))
    def _():
        arrived(first)

    fill_halo(0)
    y1 = phi(g.at[0], inv.at[0])

    @pl.when(last)
    def _():
        for i in range(bx):
            value = y1[i] + src_ref[1, i]
            adj_ref[1, i] = value
            m[H + i, core, :] = value
        for q, copy in around_m:
            start(q[1], copy)

    fill_halo(1)

    @pl.when(last)
    def _():
        arrived(around_m)
        top = phi(m, inv.at[1])
        for i in range(bx):
            c[i] = top[i] + src_ref[0, i]

    not_last = jnp.logical_not(last)

    @pl.when(not_last)
    def _():
        for j in range(blocks):
            cells = slice(j * BLOCK_CELLS, (j + 1) * BLOCK_CELLS)
            c[:, cells, :] = 1.0 / (1.0 + steps * (pick(5, j, 0) + g[1, H : H + bx, cells, :]))
        for i in range(bx):
            adj_ref[0, i] = y1[i] + src_ref[0, i]

    for i in range(chunks):
        rows = pl.ds(i * half, half)

        @pl.when(not_last)
        def _():
            mains[i].wait_recv()
            c[rows] = c[rows] * m[pl.ds(H + i * half, half), core, :] + adj_ref[0, rows]

        start(t > 0, mains[i])
    for q, copy in down:
        start(jnp.logical_and(t > 0, q[1]), copy)
    adj_ref[0] = c[...]
    saves = [
        pltpu.make_async_copy(adj_ref.at[k], adj_hbm.at[k], o_sem.at[k]) for k in range(steps)
    ]
    saves[0].start()
    loads[4].wait()
    p[...] = c[...] * fs_ref[0]

    @pl.when(not_last)
    def _():
        arrived(down)
        top = phi(m, inv.at[1])
        for i in range(bx):
            adj_ref[1, i] = top[i] + src_ref[1, i]

    p[...] = -(p[...] + adj_ref[1] * fs_ref[1])
    to_prev = pltpu.make_async_remote_copy(
        src_ref=p, dst_ref=r, send_sem=r_send.at[0], recv_sem=r_recv.at[0],
        device_id=(t - 1, sx, sy), device_id_type=MESH,
    )

    def spread(owner, k):
        return pltpu.make_async_remote_copy(
            src_ref=p, dst_ref=tot.at[owner], send_sem=t_send.at[k], recv_sem=t_recv.at[owner],
            device_id=(k, sx, sy), device_id_type=MESH,
        )

    @pl.when(jnp.logical_and(not_last, t > 0))
    def _():
        to_prev.wait_recv()
        p[...] += r[...]

    @pl.when(t >= 2)
    def _():
        to_prev.start()

    for owner in range(2):

        @pl.when(t == owner)
        def _():
            for k in range(nt - 1, -1, -1):
                if k != owner:
                    spread(owner, k).start()
            tot[owner] = p[...]

    saves[1].start()
    for owner in range(2):
        wait_in(t != owner, spread(owner, 0))
    grad_ref[...] = tot[0] + tot[1]
    save_grad = pltpu.make_async_copy(grad_ref, grad_hbm, o_sem.at[2])
    save_grad.start()

    @pl.when(t >= 2)
    def _():
        to_prev.wait_send()

    for owner in range(2):

        @pl.when(t == owner)
        def _():
            for k in range(nt):
                if k != owner:
                    spread(owner, k).wait_send()

    @pl.when(t > 0)
    def _():
        for copy in mains:
            copy.wait_send()

    @pl.when(last)
    def _():
        for q, copy in alone:
            wait_out(q[1], copy)

    @pl.when(not_last)
    def _():
        for q, copy in first:
            wait_out(q[1], copy)

    @pl.when(t == nt - 2)
    def _():
        for q, copy in up:
            wait_out(q[1], copy)

    for q, copy in second:
        wait_out(q[1], copy)
    for q, copy in around_m:
        wait_out(jnp.logical_and(last, q[1]), copy)
    for q, copy in down:
        wait_out(jnp.logical_and(t > 0, q[1]), copy)
    for save in saves:
        save.wait()
    save_grad.wait()


def shards(sources, forward_states, terminal, damping, contact_stiff, regions):
    nt, ns = lax.axis_size("tm"), lax.axis_size("sx")
    steps, bx, by, cz = sources.shape
    assert nt > 2 and steps == 2 and bx == BLOCK_CELLS and lax.axis_size("sy") == 2
    hbm = pl.BlockSpec(memory_space=pltpu.HBM)
    f32 = jnp.float32
    ext = (bx + 2 * H, by + HY, cz)
    block = (bx, by, cz)
    dma = pltpu.SemaphoreType.DMA
    return pl.pallas_call(
        functools.partial(kernel, nt, ns),
        out_shape=(
            jax.ShapeDtypeStruct(sources.shape, f32),
            jax.ShapeDtypeStruct(block, f32),
        ),
        in_specs=[hbm] * 6,
        out_specs=(hbm, hbm),
        scratch_shapes=[
            pltpu.VMEM(sources.shape, f32),
            pltpu.VMEM(block, f32),
            pltpu.VMEM(sources.shape, f32),
            pltpu.VMEM(sources.shape, f32),
            pltpu.SMEM(contact_stiff.shape, f32),
            pltpu.SMEM(regions.shape, jnp.int32),
            pltpu.VMEM((6, 8, cz), f32),
            pltpu.VMEM((2,) + ext, f32),
            pltpu.VMEM((2,) + ext, f32),
            pltpu.VMEM(ext, f32),
            pltpu.VMEM(ext, f32),
            pltpu.VMEM(ext, f32),
            pltpu.VMEM(block, f32),
            pltpu.VMEM(block, f32),
            pltpu.VMEM(block, f32),
            pltpu.VMEM((2,) + block, f32),
            dma((6,)), dma((3,)), dma((5,)), dma((5,)), dma((5,)), dma((5,)), dma((5,)), dma((5,)), dma((5,)),
            dma((9,)), dma((9,)), dma((1,)), dma((1,)), dma((nt,)), dma((2,)),
        ],
        compiler_params=pltpu.CompilerParams(
            collective_id=0, has_side_effects=True, vmem_limit_bytes=64 * 1024 * 1024
        ),
    )(sources, forward_states, terminal, damping, contact_stiff, regions)


def solution(mesh):
    in_specs = (
        P("tm", "sx", "sy", None),
        P("tm", "sx", "sy", None),
        P("sx", "sy", None),
        P("sx", "sy", None),
        P(),
        P("tm", "sx", "sy"),
    )
    out_specs = (P("tm", "sx", "sy", None), P("sx", "sy", None))
    return jax.shard_map(shards, mesh=mesh, in_specs=in_specs, out_specs=out_specs, check_vma=False)
```

```python
import functools

import jax
import jax.numpy as jnp
from jax import lax
from jax.experimental import pallas as pl
from jax.experimental.pallas import tpu as pltpu
from jax.sharding import PartitionSpec as P

MESH = pl.DeviceIdType.MESH
SWEEPS = 4
BLOCK_CELLS = 8
COUPLING = 0.5
H = SWEEPS
HY = 8

XLO, XHI, YS, CLO, CHI, MAIN0, MAIN1 = range(7)


def kernel(
    nt, ns, src_hbm, fs_hbm, term_hbm, damp_hbm, stiff_hbm, reg_hbm,
    adj_hbm, grad_hbm,
    adj_ref, grad_ref, src_ref, fs_ref, stiff_ref, reg_ref, picks, inv,
    g, m, xa, xb, c, r, p, tot,
    l_sem, o_sem, g_send, g_recv, h_send, h_recv, u_send, m_send, m_recv, r_send, r_recv, t_send, t_recv,
):
    steps, bx, by, cz = src_ref.shape
    ex, ey = bx + 2 * H, by + HY
    t = lax.axis_index("tm")
    sx = lax.axis_index("sx")
    sy = lax.axis_index("sy")
    last = t == nt - 1
    other = 1 - sy
    has_lo, has_hi = sx > 0, sx < ns - 1
    always = t >= 0
    ys = pl.multiple_of(other * HY, HY)

    core = pl.ds(0, by)
    edge = pl.ds(ys, HY)
    far = pl.ds(by, HY)
    pieces = [
        (XHI, has_lo, sx - 1, sy, (0, H), H + bx, core, core),
        (XLO, has_hi, sx + 1, sy, (bx - H, bx), 0, core, core),
        (YS, always, sx, other, (0, bx), H, edge, far),
        (CHI, has_lo, sx - 1, other, (0, H - 1), H + bx, edge, far),
        (CLO, has_hi, sx + 1, other, (bx - H + 1, bx), 1, edge, far),
    ]
    arrives = {XLO: has_lo, XHI: has_hi, YS: always, CLO: has_lo, CHI: has_hi}

    body = pl.ds(H, bx)
    own = g.at[0, body, core]
    loads = [
        pltpu.make_async_copy(stiff_hbm, stiff_ref, l_sem.at[0]),
        pltpu.make_async_copy(reg_hbm, reg_ref, l_sem.at[1]),
        pltpu.make_async_copy(damp_hbm, g.at[1, body, core], l_sem.at[2]),
        pltpu.make_async_copy(src_hbm, src_ref, l_sem.at[3]),
        pltpu.make_async_copy(fs_hbm, fs_ref, l_sem.at[4]),
    ]
    from_term = pltpu.make_async_copy(term_hbm, own, l_sem.at[5])
    from_src = pltpu.make_async_copy(src_hbm.at[1], own, l_sem.at[5])
    for load in loads[:3]:
        load.start()

    @pl.when(t == nt - 1)
    def _():
        from_term.start()

    @pl.when(t != nt - 1)
    def _():
        from_src.start()

    for load in loads[3:]:
        load.start()

    edge_zero = jnp.zeros((H, ey, cz), jnp.float32)
    far_zero = jnp.zeros((bx, HY, cz), jnp.float32)
    for ref in (g.at[0], g.at[1], m):
        ref[0:H] = edge_zero
        ref[H + bx : ex] = edge_zero
        ref[H : H + bx, by:ey] = far_zero

    barrier = pltpu.get_barrier_semaphore()

    def greet(cond, dev):
        @pl.when(cond)
        def _():
            pl.semaphore_signal(barrier, inc=1, device_id=dev, device_id_type=MESH)

    for slot, cond, dx, dy, *_ in pieces:
        greet(cond, (t, dx, dy))
    for dt, cond_t in ((t - 1, t > 0), (t + 1, t < nt - 1)):
        greet(cond_t, (dt, sx, sy))
        for slot, cond, dx, dy, *_ in pieces:
            greet(jnp.logical_and(cond_t, cond), (dt, dx, dy))
    for owner in range(2):
        greet(t > owner + 1, (owner, sx, sy))
        for k in range(owner + 2, nt):
            greet(t == owner, (k, sx, sy))
    one = lambda cond: jnp.where(cond, 1, 0)
    around = 2 * (one(has_lo) + one(has_hi)) + 1
    slabs = one(t > 0) + one(t < nt - 1)
    friends = around + slabs * (around + 1) + one(t > 1) + one(t > 2)
    friends += one(t == 0) * (nt - 2) + one(t == 1) * (nt - 3)

    blocks = by // BLOCK_CELLS
    for load in loads[:2]:
        load.wait()
    late = jnp.where(last, 1, 0)
    for j in range(blocks):
        for k, step in enumerate((late, 1 - late)):
            value = stiff_ref[reg_ref[step, 0, j]]
            picks[5, j * steps + k : j * steps + k + 1, :] = jnp.full((1, cz), value, jnp.float32)

    def piece_copy(piece, src, off, dst, dt, send, recv, fields=None):
        slot, cond, dx, dy, (lo, hi), to, ysrc, ydst = piece
        s_at = (pl.ds(off + lo, hi - lo), ysrc)
        d_at = (pl.ds(to, hi - lo), ydst)
        if fields is not None:
            s_at, d_at = (fields,) + s_at, (fields,) + d_at
        return pltpu.make_async_remote_copy(
            src_ref=src.at[s_at], dst_ref=dst.at[d_at],
            send_sem=send.at[slot], recv_sem=recv.at[slot],
            device_id=(dt, dx, dy), device_id_type=MESH,
        )

    def start(cond, copy):
        @pl.when(cond)
        def _():
            copy.start()

    def wait_in(cond, copy):
        @pl.when(cond)
        def _():
            copy.wait_recv()

    def wait_out(cond, copy):
        @pl.when(cond)
        def _():
            copy.wait_send()

    first = [(q, piece_copy(q, g, H, g, t, g_send, g_recv, pl.ds(0, 2))) for q in pieces]
    second = [
        (
            q,
            pltpu.make_async_remote_copy(
                src_ref=picks.at[5], dst_ref=picks.at[q[0]],
                send_sem=h_send.at[q[0]], recv_sem=h_recv.at[q[0]],
                device_id=(t, q[2], q[3]), device_id_type=MESH,
            ),
        )
        for q in pieces
    ]
    around_m = [(q, piece_copy(q, m, H, m, t, u_send, m_recv)) for q in pieces]
    down = [(q, piece_copy(q, c, 0, m, t - 1, m_send, m_recv)) for q in pieces]
    chunks = 4
    half = bx // chunks
    mains = [
        pltpu.make_async_remote_copy(
            src_ref=c.at[pl.ds(i * half, half)], dst_ref=m.at[pl.ds(H + i * half, half), core],
            send_sem=m_send.at[MAIN0 + i], recv_sem=m_recv.at[MAIN0 + i],
            device_id=(t - 1, sx, sy), device_id_type=MESH,
        )
        for i in range(chunks)
    ]

    pl.semaphore_wait(barrier, friends)
    loads[2].wait()

    from_src.wait()
    for q, copy in first:
        start(q[1], copy)
    for q, copy in second:
        start(q[1], copy)

    lane = lax.broadcasted_iota(jnp.int32, (ey, cz), 1)
    row = lax.broadcasted_iota(jnp.int32, (ey, cz), 0)
    no_before = jnp.logical_and(row == 0, sy == 0)
    no_after = jnp.logical_and(row == by - 1, sy == 1)
    z_first, z_last = lane == 0, lane == cz - 1

    def phi(b, inv):
        bufs = [b, xa, xb]
        cur = b
        out = []
        for s in range(1, SWEEPS + 1):
            nxt = xa if s % 2 else xb
            for i in range(s, ex - s):
                x = cur[i]
                total = cur[i - 1] + cur[i + 1]
                total += jnp.where(no_before, 0.0, pltpu.roll(x, 1, 0))
                total += jnp.where(no_after, 0.0, pltpu.roll(x, ey - 1, 0))
                total += jnp.where(z_first, 0.0, pltpu.roll(x, 1, 1))
                total += jnp.where(z_last, 0.0, pltpu.roll(x, cz - 1, 1))
                value = (b[i] + COUPLING * total) * inv[i]
                if s == SWEEPS:
                    out.append(value[:by])
                else:
                    nxt[i] = value
            cur = nxt
        return out

    def arrived(copies):
        for q, copy in copies:
            wait_in(arrives[q[0]], copy)

    def pick(slot, j, k):
        return picks[slot, j * steps + k : j * steps + k + 1, :]

    def near_pick(slot, k):
        if blocks == 1:
            return pick(slot, 0, k)
        return jnp.where(sy == 1, pick(slot, blocks - 1, k), pick(slot, 0, k))

    def inverse(at, i, cells):
        return 1.0 / (1.0 + (at + g[1, i, cells, :]) + 6.0 * COUPLING)

    def fill_own(out):
        for i in range(H, H + bx):
            for j in range(blocks):
                cells = slice(j * BLOCK_CELLS, (j + 1) * BLOCK_CELLS)
                inv[out, i, cells, :] = inverse(pick(5, j, out), i, cells)

    def fill_halo(out):
        for rows, straight, corner, inside in (
            (range(1, H), XLO, CLO, has_lo),
            (range(H + bx, ex - 1), XHI, CHI, has_hi),
        ):
            for i in rows:
                for j in range(blocks):
                    cells = slice(j * BLOCK_CELLS, (j + 1) * BLOCK_CELLS)
                    value = inverse(pick(straight, j, out), i, cells)
                    inv[out, i, cells, :] = jnp.where(inside, value, 0.0)
                value = inverse(near_pick(corner, out), i, slice(by, ey))
                inv[out, i, by:ey, :] = jnp.where(inside, value, 0.0)
        for i in range(H, H + bx):
            inv[out, i, by:ey, :] = inverse(near_pick(YS, out), i, slice(by, ey))

    fill_own(0)
    fill_own(1)
    loads[3].wait()
    arrived(second)
    arrived(first)
    fill_halo(0)
    y1 = phi(g.at[0], inv.at[0])

    @pl.when(last)
    def _():
        for i in range(bx):
            value = y1[i] + src_ref[1, i]
            adj_ref[1, i] = value
            m[H + i, core, :] = value
        for q, copy in around_m:
            start(q[1], copy)

    fill_halo(1)

    @pl.when(last)
    def _():
        arrived(around_m)
        top = phi(m, inv.at[1])
        for i in range(bx):
            c[i] = top[i] + src_ref[0, i]

    not_last = jnp.logical_not(last)

    @pl.when(not_last)
    def _():
        for j in range(blocks):
            cells = slice(j * BLOCK_CELLS, (j + 1) * BLOCK_CELLS)
            c[:, cells, :] = 1.0 / (1.0 + steps * (pick(5, j, 0) + g[1, H : H + bx, cells, :]))
        for i in range(bx):
            adj_ref[0, i] = y1[i] + src_ref[0, i]

    for i in range(chunks):
        rows = pl.ds(i * half, half)

        @pl.when(not_last)
        def _():
            mains[i].wait_recv()
            c[rows] = c[rows] * m[pl.ds(H + i * half, half), core, :] + adj_ref[0, rows]

        start(t > 0, mains[i])
    for q, copy in down:
        start(jnp.logical_and(t > 0, q[1]), copy)
    adj_ref[0] = c[...]
    saves = [
        pltpu.make_async_copy(adj_ref.at[k], adj_hbm.at[k], o_sem.at[k]) for k in range(steps)
    ]
    saves[0].start()
    loads[4].wait()
    p[...] = c[...] * fs_ref[0]

    @pl.when(not_last)
    def _():
        arrived(down)
        top = phi(m, inv.at[1])
        for i in range(bx):
            adj_ref[1, i] = top[i] + src_ref[1, i]

    p[...] = -(p[...] + adj_ref[1] * fs_ref[1])
    to_prev = pltpu.make_async_remote_copy(
        src_ref=p, dst_ref=r, send_sem=r_send.at[0], recv_sem=r_recv.at[0],
        device_id=(t - 1, sx, sy), device_id_type=MESH,
    )

    def spread(owner, k):
        return pltpu.make_async_remote_copy(
            src_ref=p, dst_ref=tot.at[owner], send_sem=t_send.at[k], recv_sem=t_recv.at[owner],
            device_id=(k, sx, sy), device_id_type=MESH,
        )

    @pl.when(jnp.logical_and(not_last, t > 0))
    def _():
        to_prev.wait_recv()
        p[...] += r[...]

    @pl.when(t >= 2)
    def _():
        to_prev.start()

    for owner in range(2):

        @pl.when(t == owner)
        def _():
            for k in range(nt - 1, -1, -1):
                if k != owner:
                    spread(owner, k).start()
            tot[owner] = p[...]

    saves[1].start()
    for q, copy in first + second:
        wait_out(q[1], copy)
    for q, copy in around_m:
        wait_out(jnp.logical_and(last, q[1]), copy)

    @pl.when(t > 0)
    def _():
        for copy in mains:
            copy.wait_send()
        for q, copy in down:
            wait_out(q[1], copy)

    @pl.when(t >= 2)
    def _():
        to_prev.wait_send()

    saves[0].wait()
    for owner in range(2):
        wait_in(t != owner, spread(owner, 0))
    grad_ref[...] = tot[0] + tot[1]
    save_grad = pltpu.make_async_copy(grad_ref, grad_hbm, o_sem.at[2])
    save_grad.start()

    for owner in range(2):

        @pl.when(t == owner)
        def _():
            for k in range(nt):
                if k != owner:
                    spread(owner, k).wait_send()

    saves[1].wait()
    save_grad.wait()


def shards(sources, forward_states, terminal, damping, contact_stiff, regions):
    nt, ns = lax.axis_size("tm"), lax.axis_size("sx")
    steps, bx, by, cz = sources.shape
    assert nt > 2 and steps == 2 and bx == BLOCK_CELLS and lax.axis_size("sy") == 2
    hbm = pl.BlockSpec(memory_space=pltpu.HBM)
    f32 = jnp.float32
    ext = (bx + 2 * H, by + HY, cz)
    block = (bx, by, cz)
    dma = pltpu.SemaphoreType.DMA
    return pl.pallas_call(
        functools.partial(kernel, nt, ns),
        out_shape=(
            jax.ShapeDtypeStruct(sources.shape, f32),
            jax.ShapeDtypeStruct(block, f32),
        ),
        in_specs=[hbm] * 6,
        out_specs=(hbm, hbm),
        scratch_shapes=[
            pltpu.VMEM(sources.shape, f32),
            pltpu.VMEM(block, f32),
            pltpu.VMEM(sources.shape, f32),
            pltpu.VMEM(sources.shape, f32),
            pltpu.SMEM(contact_stiff.shape, f32),
            pltpu.SMEM(regions.shape, jnp.int32),
            pltpu.VMEM((6, 8, cz), f32),
            pltpu.VMEM((2,) + ext, f32),
            pltpu.VMEM((2,) + ext, f32),
            pltpu.VMEM(ext, f32),
            pltpu.VMEM(ext, f32),
            pltpu.VMEM(ext, f32),
            pltpu.VMEM(block, f32),
            pltpu.VMEM(block, f32),
            pltpu.VMEM(block, f32),
            pltpu.VMEM((2,) + block, f32),
            dma((6,)), dma((3,)), dma((5,)), dma((5,)), dma((5,)), dma((5,)), dma((5,)),
            dma((9,)), dma((9,)), dma((1,)), dma((1,)), dma((nt,)), dma((2,)),
        ],
        compiler_params=pltpu.CompilerParams(
            collective_id=0, has_side_effects=True, vmem_limit_bytes=64 * 1024 * 1024
        ),
    )(sources, forward_states, terminal, damping, contact_stiff, regions)


def solution(mesh):
    in_specs = (
        P("tm", "sx", "sy", None),
        P("tm", "sx", "sy", None),
        P("sx", "sy", None),
        P("sx", "sy", None),
        P(),
        P("tm", "sx", "sy"),
    )
    out_specs = (P("tm", "sx", "sy", None), P("sx", "sy", None))
    return jax.shard_map(shards, mesh=mesh, in_specs=in_specs, out_specs=out_specs, check_vma=False)
```

```python
import functools

import jax
import jax.numpy as jnp
from jax import lax
from jax.experimental import pallas as pl
from jax.experimental.pallas import tpu as pltpu
from jax.sharding import PartitionSpec as P

MESH = pl.DeviceIdType.MESH
SWEEPS = 4
BLOCK_CELLS = 8
COUPLING = 0.5
H = SWEEPS
HY = 8

XLO, XHI, YS, CLO, CHI, MAIN0, MAIN1 = range(7)


def kernel(
    nt, ns, src_hbm, fs_hbm, term_hbm, damp_hbm, stiff_hbm, reg_hbm,
    adj_hbm, grad_hbm,
    adj_ref, grad_ref, src_ref, fs_ref, stiff_ref, reg_ref, picks, inv,
    g, m, xa, xb, c, r, p, tot,
    l_sem, o_sem, g_send, g_recv, h_send, h_recv, u_send, m_send, m_recv, r_send, r_recv, t_send, t_recv,
):
    steps, bx, by, cz = src_ref.shape
    ex, ey = bx + 2 * H, by + HY
    t = lax.axis_index("tm")
    sx = lax.axis_index("sx")
    sy = lax.axis_index("sy")
    last = t == nt - 1
    other = 1 - sy
    has_lo, has_hi = sx > 0, sx < ns - 1
    always = t >= 0
    ys = pl.multiple_of(other * HY, HY)

    core = pl.ds(0, by)
    edge = pl.ds(ys, HY)
    far = pl.ds(by, HY)
    pieces = [
        (XHI, has_lo, sx - 1, sy, (0, H), H + bx, core, core),
        (XLO, has_hi, sx + 1, sy, (bx - H, bx), 0, core, core),
        (YS, always, sx, other, (0, bx), H, edge, far),
        (CHI, has_lo, sx - 1, other, (0, H - 1), H + bx, edge, far),
        (CLO, has_hi, sx + 1, other, (bx - H + 1, bx), 1, edge, far),
    ]
    arrives = {XLO: has_lo, XHI: has_hi, YS: always, CLO: has_lo, CHI: has_hi}

    body = pl.ds(H, bx)
    own = g.at[0, body, core]
    loads = [
        pltpu.make_async_copy(stiff_hbm, stiff_ref, l_sem.at[0]),
        pltpu.make_async_copy(reg_hbm, reg_ref, l_sem.at[1]),
        pltpu.make_async_copy(damp_hbm, g.at[1, body, core], l_sem.at[2]),
        pltpu.make_async_copy(src_hbm, src_ref, l_sem.at[3]),
        pltpu.make_async_copy(fs_hbm, fs_ref, l_sem.at[4]),
    ]
    from_term = pltpu.make_async_copy(term_hbm, own, l_sem.at[5])
    from_src = pltpu.make_async_copy(src_hbm.at[1], own, l_sem.at[5])
    for load in loads[:3]:
        load.start()

    @pl.when(t == nt - 1)
    def _():
        from_term.start()

    @pl.when(t != nt - 1)
    def _():
        from_src.start()

    for load in loads[3:]:
        load.start()

    edge_zero = jnp.zeros((H, ey, cz), jnp.float32)
    far_zero = jnp.zeros((bx, HY, cz), jnp.float32)
    for ref in (g.at[0], g.at[1], m):
        ref[0:H] = edge_zero
        ref[H + bx : ex] = edge_zero
        ref[H : H + bx, by:ey] = far_zero

    barrier = pltpu.get_barrier_semaphore()

    def greet(cond, dev):
        @pl.when(cond)
        def _():
            pl.semaphore_signal(barrier, inc=1, device_id=dev, device_id_type=MESH)

    for slot, cond, dx, dy, *_ in pieces:
        greet(cond, (t, dx, dy))
    for dt, cond_t in ((t - 1, t > 0), (t + 1, t < nt - 1)):
        greet(cond_t, (dt, sx, sy))
        for slot, cond, dx, dy, *_ in pieces:
            greet(jnp.logical_and(cond_t, cond), (dt, dx, dy))
    for owner in range(2):
        greet(t > owner + 1, (owner, sx, sy))
        for k in range(owner + 2, nt):
            greet(t == owner, (k, sx, sy))
    one = lambda cond: jnp.where(cond, 1, 0)
    around = 2 * (one(has_lo) + one(has_hi)) + 1
    slabs = one(t > 0) + one(t < nt - 1)
    friends = around + slabs * (around + 1) + one(t > 1) + one(t > 2)
    friends += one(t == 0) * (nt - 2) + one(t == 1) * (nt - 3)

    blocks = by // BLOCK_CELLS
    for load in loads[:2]:
        load.wait()
    late = jnp.where(t == nt - 1, 1, 0)
    for j in range(blocks):
        for k, step in enumerate((late, 1 - late)):
            value = stiff_ref[reg_ref[step, 0, j]]
            picks[5, j * steps + k : j * steps + k + 1, :] = jnp.full((1, cz), value, jnp.float32)

    def piece_copy(piece, src, off, dst, dt, send, recv, fields=None):
        slot, cond, dx, dy, (lo, hi), to, ysrc, ydst = piece
        s_at = (pl.ds(off + lo, hi - lo), ysrc)
        d_at = (pl.ds(to, hi - lo), ydst)
        if fields is not None:
            s_at, d_at = (fields,) + s_at, (fields,) + d_at
        return pltpu.make_async_remote_copy(
            src_ref=src.at[s_at], dst_ref=dst.at[d_at],
            send_sem=send.at[slot], recv_sem=recv.at[slot],
            device_id=(dt, dx, dy), device_id_type=MESH,
        )

    def start(cond, copy):
        @pl.when(cond)
        def _():
            copy.start()

    def wait_in(cond, copy):
        @pl.when(cond)
        def _():
            copy.wait_recv()

    def wait_out(cond, copy):
        @pl.when(cond)
        def _():
            copy.wait_send()

    first = [(q, piece_copy(q, g, H, g, t, g_send, g_recv, pl.ds(0, 2))) for q in pieces]
    second = [
        (
            q,
            pltpu.make_async_remote_copy(
                src_ref=picks.at[5], dst_ref=picks.at[q[0]],
                send_sem=h_send.at[q[0]], recv_sem=h_recv.at[q[0]],
                device_id=(t, q[2], q[3]), device_id_type=MESH,
            ),
        )
        for q in pieces
    ]
    around_m = [(q, piece_copy(q, m, H, m, t, u_send, m_recv)) for q in pieces]
    down = [(q, piece_copy(q, c, 0, m, t - 1, m_send, m_recv)) for q in pieces]
    chunks = 2
    half = bx // chunks
    mains = [
        pltpu.make_async_remote_copy(
            src_ref=c.at[pl.ds(i * half, half)], dst_ref=m.at[pl.ds(H + i * half, half), core],
            send_sem=m_send.at[MAIN0 + i], recv_sem=m_recv.at[MAIN0 + i],
            device_id=(t - 1, sx, sy), device_id_type=MESH,
        )
        for i in range(chunks)
    ]

    pl.semaphore_wait(barrier, friends)
    for q, copy in second:
        start(q[1], copy)
    loads[2].wait()
    from_src.wait()
    for q, copy in first:
        start(q[1], copy)

    lane = lax.broadcasted_iota(jnp.int32, (ey, cz), 1)
    row = lax.broadcasted_iota(jnp.int32, (ey, cz), 0)
    no_before = jnp.logical_and(row == 0, sy == 0)
    no_after = jnp.logical_and(row == by - 1, sy == 1)
    z_first, z_last = lane == 0, lane == cz - 1

    def phi(b, inv):
        bufs = [b, xa, xb]
        cur = b
        out = []
        for s in range(1, SWEEPS + 1):
            nxt = xa if s % 2 else xb
            for i in range(s, ex - s):
                x = cur[i]
                total = cur[i - 1] + cur[i + 1]
                total += jnp.where(no_before, 0.0, pltpu.roll(x, 1, 0))
                total += jnp.where(no_after, 0.0, pltpu.roll(x, ey - 1, 0))
                total += jnp.where(z_first, 0.0, pltpu.roll(x, 1, 1))
                total += jnp.where(z_last, 0.0, pltpu.roll(x, cz - 1, 1))
                value = (b[i] + COUPLING * total) * inv[i]
                if s == SWEEPS:
                    out.append(value[:by])
                else:
                    nxt[i] = value
            cur = nxt
        return out

    def arrived(copies):
        for q, copy in copies:
            wait_in(arrives[q[0]], copy)

    def pick(slot, j, k):
        return picks[slot, j * steps + k : j * steps + k + 1, :]

    def near_pick(slot, k):
        if blocks == 1:
            return pick(slot, 0, k)
        return jnp.where(sy == 1, pick(slot, blocks - 1, k), pick(slot, 0, k))

    def fill(out, k, rows, straight, corner, inside):
        for i in rows:
            for j in range(blocks):
                cells = slice(j * BLOCK_CELLS, (j + 1) * BLOCK_CELLS)
                value = 1.0 / (1.0 + (pick(straight, j, k) + g[1, i, cells, :]) + 6.0 * COUPLING)
                inv[out, i, cells, :] = jnp.where(inside, value, 0.0)
            value = 1.0 / (1.0 + (near_pick(corner, k) + g[1, i, by:ey, :]) + 6.0 * COUPLING)
            inv[out, i, by:ey, :] = jnp.where(inside, value, 0.0)

    def fill_all(out, k):
        fill(out, k, range(1, H), XLO, CLO, has_lo)
        fill(out, k, range(H, H + bx), 5, YS, always)
        fill(out, k, range(H + bx, ex - 1), XHI, CHI, has_hi)

    loads[3].wait()
    arrived(second)
    arrived(first)
    fill_all(0, 0)
    y1 = phi(g.at[0], inv.at[0])

    @pl.when(last)
    def _():
        for i in range(bx):
            value = y1[i] + src_ref[1, i]
            adj_ref[1, i] = value
            m[H + i, core, :] = value
        for q, copy in around_m:
            start(q[1], copy)

    fill_all(1, 1)

    @pl.when(last)
    def _():
        arrived(around_m)
        top = phi(m, inv.at[1])
        for i in range(bx):
            c[i] = top[i] + src_ref[0, i]

    not_last = jnp.logical_not(last)

    @pl.when(not_last)
    def _():
        for j in range(blocks):
            cells = slice(j * BLOCK_CELLS, (j + 1) * BLOCK_CELLS)
            c[:, cells, :] = 1.0 / (1.0 + steps * (pick(5, j, 0) + g[1, H : H + bx, cells, :]))
        for i in range(bx):
            adj_ref[0, i] = y1[i] + src_ref[0, i]

    for i in range(chunks):
        rows = pl.ds(i * half, half)

        @pl.when(not_last)
        def _():
            mains[i].wait_recv()
            c[rows] = c[rows] * m[pl.ds(H + i * half, half), core, :] + adj_ref[0, rows]

        start(t > 0, mains[i])
    for q, copy in down:
        start(jnp.logical_and(t > 0, q[1]), copy)
    adj_ref[0] = c[...]
    saves = [
        pltpu.make_async_copy(adj_ref.at[k], adj_hbm.at[k], o_sem.at[k]) for k in range(steps)
    ]
    saves[0].start()
    loads[4].wait()
    p[...] = c[...] * fs_ref[0]

    @pl.when(not_last)
    def _():
        arrived(down)
        top = phi(m, inv.at[1])
        for i in range(bx):
            adj_ref[1, i] = top[i] + src_ref[1, i]

    p[...] = -(p[...] + adj_ref[1] * fs_ref[1])
    to_prev = pltpu.make_async_remote_copy(
        src_ref=p, dst_ref=r, send_sem=r_send.at[0], recv_sem=r_recv.at[0],
        device_id=(t - 1, sx, sy), device_id_type=MESH,
    )

    def spread(owner, k):
        return pltpu.make_async_remote_copy(
            src_ref=p, dst_ref=tot.at[owner], send_sem=t_send.at[k], recv_sem=t_recv.at[owner],
            device_id=(k, sx, sy), device_id_type=MESH,
        )

    @pl.when(jnp.logical_and(not_last, t > 0))
    def _():
        to_prev.wait_recv()
        p[...] += r[...]

    @pl.when(t >= 2)
    def _():
        to_prev.start()

    for owner in range(2):

        @pl.when(t == owner)
        def _():
            for k in range(nt - 1, -1, -1):
                if k != owner:
                    spread(owner, k).start()
            tot[owner] = p[...]

    saves[1].start()
    for owner in range(2):
        wait_in(t != owner, spread(owner, 0))
    grad_ref[...] = tot[0] + tot[1]
    save_grad = pltpu.make_async_copy(grad_ref, grad_hbm, o_sem.at[2])
    save_grad.start()

    @pl.when(t >= 2)
    def _():
        to_prev.wait_send()

    for owner in range(2):

        @pl.when(t == owner)
        def _():
            for k in range(nt):
                if k != owner:
                    spread(owner, k).wait_send()

    @pl.when(t > 0)
    def _():
        for copy in mains:
            copy.wait_send()

    for q, copy in first + second:
        wait_out(q[1], copy)
    for q, copy in around_m:
        wait_out(jnp.logical_and(last, q[1]), copy)
    for q, copy in down:
        wait_out(jnp.logical_and(t > 0, q[1]), copy)
    for save in saves:
        save.wait()
    save_grad.wait()


def shards(sources, forward_states, terminal, damping, contact_stiff, regions):
    nt, ns = lax.axis_size("tm"), lax.axis_size("sx")
    steps, bx, by, cz = sources.shape
    assert nt > 2 and steps == 2 and bx == BLOCK_CELLS and lax.axis_size("sy") == 2
    hbm = pl.BlockSpec(memory_space=pltpu.HBM)
    f32 = jnp.float32
    ext = (bx + 2 * H, by + HY, cz)
    block = (bx, by, cz)
    dma = pltpu.SemaphoreType.DMA
    return pl.pallas_call(
        functools.partial(kernel, nt, ns),
        out_shape=(
            jax.ShapeDtypeStruct(sources.shape, f32),
            jax.ShapeDtypeStruct(block, f32),
        ),
        in_specs=[hbm] * 6,
        out_specs=(hbm, hbm),
        scratch_shapes=[
            pltpu.VMEM(sources.shape, f32),
            pltpu.VMEM(block, f32),
            pltpu.VMEM(sources.shape, f32),
            pltpu.VMEM(sources.shape, f32),
            pltpu.SMEM(contact_stiff.shape, f32),
            pltpu.SMEM(regions.shape, jnp.int32),
            pltpu.VMEM((6, 8, cz), f32),
            pltpu.VMEM((2,) + ext, f32),
            pltpu.VMEM((2,) + ext, f32),
            pltpu.VMEM(ext, f32),
            pltpu.VMEM(ext, f32),
            pltpu.VMEM(ext, f32),
            pltpu.VMEM(block, f32),
            pltpu.VMEM(block, f32),
            pltpu.VMEM(block, f32),
            pltpu.VMEM((2,) + block, f32),
            dma((6,)), dma((3,)), dma((5,)), dma((5,)), dma((5,)), dma((5,)), dma((5,)),
            dma((9,)), dma((9,)), dma((1,)), dma((1,)), dma((nt,)), dma((2,)),
        ],
        compiler_params=pltpu.CompilerParams(
            collective_id=0, has_side_effects=True, vmem_limit_bytes=64 * 1024 * 1024
        ),
    )(sources, forward_states, terminal, damping, contact_stiff, regions)


def solution(mesh):
    in_specs = (
        P("tm", "sx", "sy", None),
        P("tm", "sx", "sy", None),
        P("sx", "sy", None),
        P("sx", "sy", None),
        P(),
        P("tm", "sx", "sy"),
    )
    out_specs = (P("tm", "sx", "sy", None), P("sx", "sy", None))
    return jax.shard_map(shards, mesh=mesh, in_specs=in_specs, out_specs=out_specs, check_vma=False)
```

```python
import functools

import jax
import jax.numpy as jnp
from jax import lax
from jax.experimental import pallas as pl
from jax.experimental.pallas import tpu as pltpu
from jax.sharding import PartitionSpec as P

MESH = pl.DeviceIdType.MESH
SWEEPS = 4
BLOCK_CELLS = 8
COUPLING = 0.5
H = SWEEPS
HY = 8

XLO, XHI, YS, CLO, CHI, MAIN0, MAIN1 = range(7)


def kernel(
    nt, ns, src_hbm, fs_hbm, term_hbm, damp_hbm, stiff_hbm, reg_hbm,
    adj_hbm, grad_hbm,
    adj_ref, grad_ref, src_ref, fs_ref, stiff_ref, reg_ref, picks, inv,
    g, m, xa, xb, c, r, p, tot,
    l_sem, o_sem, g_send, g_recv, h_send, h_recv, u_send, m_send, m_recv, r_send, r_recv, t_send, t_recv,
):
    steps, bx, by, cz = src_ref.shape
    ex, ey = bx + 2 * H, by + HY
    t = lax.axis_index("tm")
    sx = lax.axis_index("sx")
    sy = lax.axis_index("sy")
    last = t == nt - 1
    other = 1 - sy
    has_lo, has_hi = sx > 0, sx < ns - 1
    always = t >= 0
    ys = pl.multiple_of(other * HY, HY)

    core = pl.ds(0, by)
    edge = pl.ds(ys, HY)
    far = pl.ds(by, HY)
    pieces = [
        (XHI, has_lo, sx - 1, sy, (0, H), H + bx, core, core),
        (XLO, has_hi, sx + 1, sy, (bx - H, bx), 0, core, core),
        (YS, always, sx, other, (0, bx), H, edge, far),
        (CHI, has_lo, sx - 1, other, (0, H - 1), H + bx, edge, far),
        (CLO, has_hi, sx + 1, other, (bx - H + 1, bx), 1, edge, far),
    ]
    arrives = {XLO: has_lo, XHI: has_hi, YS: always, CLO: has_lo, CHI: has_hi}

    body = pl.ds(H, bx)
    own = g.at[0, body, core]
    loads = [
        pltpu.make_async_copy(stiff_hbm, stiff_ref, l_sem.at[0]),
        pltpu.make_async_copy(reg_hbm, reg_ref, l_sem.at[1]),
        pltpu.make_async_copy(damp_hbm, g.at[1, body, core], l_sem.at[2]),
        pltpu.make_async_copy(src_hbm, src_ref, l_sem.at[3]),
        pltpu.make_async_copy(fs_hbm, fs_ref, l_sem.at[4]),
    ]
    from_term = pltpu.make_async_copy(term_hbm, own, l_sem.at[5])
    from_src = pltpu.make_async_copy(src_hbm.at[1], own, l_sem.at[5])
    for load in loads[:3]:
        load.start()

    @pl.when(t == nt - 1)
    def _():
        from_term.start()

    @pl.when(t != nt - 1)
    def _():
        from_src.start()

    for load in loads[3:]:
        load.start()

    edge_zero = jnp.zeros((H, ey, cz), jnp.float32)
    far_zero = jnp.zeros((bx, HY, cz), jnp.float32)
    for ref in (g.at[0], g.at[1], m):
        ref[0:H] = edge_zero
        ref[H + bx : ex] = edge_zero
        ref[H : H + bx, by:ey] = far_zero

    barrier = pltpu.get_barrier_semaphore()

    def greet(cond, dev):
        @pl.when(cond)
        def _():
            pl.semaphore_signal(barrier, inc=1, device_id=dev, device_id_type=MESH)

    for slot, cond, dx, dy, *_ in pieces:
        greet(cond, (t, dx, dy))
    for dt, cond_t in ((t - 1, t > 0), (t + 1, t < nt - 1)):
        greet(cond_t, (dt, sx, sy))
        for slot, cond, dx, dy, *_ in pieces:
            greet(jnp.logical_and(cond_t, cond), (dt, dx, dy))
    for owner in range(2):
        greet(t > owner + 1, (owner, sx, sy))
        for k in range(owner + 2, nt):
            greet(t == owner, (k, sx, sy))
    one = lambda cond: jnp.where(cond, 1, 0)
    around = 2 * (one(has_lo) + one(has_hi)) + 1
    slabs = one(t > 0) + one(t < nt - 1)
    friends = around + slabs * (around + 1) + one(t > 1) + one(t > 2)
    friends += one(t == 0) * (nt - 2) + one(t == 1) * (nt - 3)

    blocks = by // BLOCK_CELLS
    for load in loads[:2]:
        load.wait()
    late = jnp.where(t == nt - 1, 1, 0)
    for j in range(blocks):
        for k, step in enumerate((late, 1 - late)):
            value = stiff_ref[reg_ref[step, 0, j]]
            picks[5, j * steps + k : j * steps + k + 1, :] = jnp.full((1, cz), value, jnp.float32)

    def piece_copy(piece, src, off, dst, dt, send, recv, fields=None):
        slot, cond, dx, dy, (lo, hi), to, ysrc, ydst = piece
        s_at = (pl.ds(off + lo, hi - lo), ysrc)
        d_at = (pl.ds(to, hi - lo), ydst)
        if fields is not None:
            s_at, d_at = (fields,) + s_at, (fields,) + d_at
        return pltpu.make_async_remote_copy(
            src_ref=src.at[s_at], dst_ref=dst.at[d_at],
            send_sem=send.at[slot], recv_sem=recv.at[slot],
            device_id=(dt, dx, dy), device_id_type=MESH,
        )

    def start(cond, copy):
        @pl.when(cond)
        def _():
            copy.start()

    def wait_in(cond, copy):
        @pl.when(cond)
        def _():
            copy.wait_recv()

    def wait_out(cond, copy):
        @pl.when(cond)
        def _():
            copy.wait_send()

    first = [(q, piece_copy(q, g, H, g, t, g_send, g_recv, pl.ds(0, 2))) for q in pieces]
    second = [
        (
            q,
            pltpu.make_async_remote_copy(
                src_ref=picks.at[5], dst_ref=picks.at[q[0]],
                send_sem=h_send.at[q[0]], recv_sem=h_recv.at[q[0]],
                device_id=(t, q[2], q[3]), device_id_type=MESH,
            ),
        )
        for q in pieces
    ]
    around_m = [(q, piece_copy(q, m, H, m, t, u_send, m_recv)) for q in pieces]
    down = [(q, piece_copy(q, c, 0, m, t - 1, m_send, m_recv)) for q in pieces]
    chunks = 8
    half = bx // chunks
    mains = [
        pltpu.make_async_remote_copy(
            src_ref=c.at[pl.ds(i * half, half)], dst_ref=m.at[pl.ds(H + i * half, half), core],
            send_sem=m_send.at[MAIN0 + i], recv_sem=m_recv.at[MAIN0 + i],
            device_id=(t - 1, sx, sy), device_id_type=MESH,
        )
        for i in range(chunks)
    ]

    pl.semaphore_wait(barrier, friends)
    for q, copy in second:
        start(q[1], copy)
    loads[2].wait()
    from_src.wait()
    for q, copy in first:
        start(q[1], copy)

    lane = lax.broadcasted_iota(jnp.int32, (ey, cz), 1)
    row = lax.broadcasted_iota(jnp.int32, (ey, cz), 0)
    no_before = jnp.logical_and(row == 0, sy == 0)
    no_after = jnp.logical_and(row == by - 1, sy == 1)
    z_first, z_last = lane == 0, lane == cz - 1

    def phi(b, inv):
        bufs = [b, xa, xb]
        cur = b
        out = []
        for s in range(1, SWEEPS + 1):
            nxt = xa if s % 2 else xb
            for i in range(s, ex - s):
                x = cur[i]
                total = cur[i - 1] + cur[i + 1]
                total += jnp.where(no_before, 0.0, pltpu.roll(x, 1, 0))
                total += jnp.where(no_after, 0.0, pltpu.roll(x, ey - 1, 0))
                total += jnp.where(z_first, 0.0, pltpu.roll(x, 1, 1))
                total += jnp.where(z_last, 0.0, pltpu.roll(x, cz - 1, 1))
                value = (b[i] + COUPLING * total) * inv[i]
                if s == SWEEPS:
                    out.append(value[:by])
                else:
                    nxt[i] = value
            cur = nxt
        return out

    def arrived(copies):
        for q, copy in copies:
            wait_in(arrives[q[0]], copy)

    def pick(slot, j, k):
        return picks[slot, j * steps + k : j * steps + k + 1, :]

    def near_pick(slot, k):
        if blocks == 1:
            return pick(slot, 0, k)
        return jnp.where(sy == 1, pick(slot, blocks - 1, k), pick(slot, 0, k))

    def fill(out, k, rows, straight, corner, inside):
        for i in rows:
            for j in range(blocks):
                cells = slice(j * BLOCK_CELLS, (j + 1) * BLOCK_CELLS)
                value = 1.0 / (1.0 + (pick(straight, j, k) + g[1, i, cells, :]) + 6.0 * COUPLING)
                inv[out, i, cells, :] = jnp.where(inside, value, 0.0)
            value = 1.0 / (1.0 + (near_pick(corner, k) + g[1, i, by:ey, :]) + 6.0 * COUPLING)
            inv[out, i, by:ey, :] = jnp.where(inside, value, 0.0)

    def fill_all(out, k):
        fill(out, k, range(1, H), XLO, CLO, has_lo)
        fill(out, k, range(H, H + bx), 5, YS, always)
        fill(out, k, range(H + bx, ex - 1), XHI, CHI, has_hi)

    loads[3].wait()
    arrived(second)
    arrived(first)
    fill_all(0, 0)
    y1 = phi(g.at[0], inv.at[0])

    @pl.when(last)
    def _():
        for i in range(bx):
            value = y1[i] + src_ref[1, i]
            adj_ref[1, i] = value
            m[H + i, core, :] = value
        for q, copy in around_m:
            start(q[1], copy)

    fill_all(1, 1)

    @pl.when(last)
    def _():
        arrived(around_m)
        top = phi(m, inv.at[1])
        for i in range(bx):
            c[i] = top[i] + src_ref[0, i]

    not_last = jnp.logical_not(last)

    @pl.when(not_last)
    def _():
        for j in range(blocks):
            cells = slice(j * BLOCK_CELLS, (j + 1) * BLOCK_CELLS)
            c[:, cells, :] = 1.0 / (1.0 + steps * (pick(5, j, 0) + g[1, H : H + bx, cells, :]))
        for i in range(bx):
            adj_ref[0, i] = y1[i] + src_ref[0, i]

    for i in range(chunks):
        rows = pl.ds(i * half, half)

        @pl.when(not_last)
        def _():
            mains[i].wait_recv()
            c[rows] = c[rows] * m[pl.ds(H + i * half, half), core, :] + adj_ref[0, rows]

        start(t > 0, mains[i])
    for q, copy in down:
        start(jnp.logical_and(t > 0, q[1]), copy)
    adj_ref[0] = c[...]
    saves = [
        pltpu.make_async_copy(adj_ref.at[k], adj_hbm.at[k], o_sem.at[k]) for k in range(steps)
    ]
    saves[0].start()
    loads[4].wait()
    p[...] = c[...] * fs_ref[0]

    @pl.when(not_last)
    def _():
        arrived(down)
        top = phi(m, inv.at[1])
        for i in range(bx):
            adj_ref[1, i] = top[i] + src_ref[1, i]

    p[...] = -(p[...] + adj_ref[1] * fs_ref[1])
    to_prev = pltpu.make_async_remote_copy(
        src_ref=p, dst_ref=r, send_sem=r_send.at[0], recv_sem=r_recv.at[0],
        device_id=(t - 1, sx, sy), device_id_type=MESH,
    )

    def spread(owner, k):
        return pltpu.make_async_remote_copy(
            src_ref=p, dst_ref=tot.at[owner], send_sem=t_send.at[k], recv_sem=t_recv.at[owner],
            device_id=(k, sx, sy), device_id_type=MESH,
        )

    @pl.when(jnp.logical_and(not_last, t > 0))
    def _():
        to_prev.wait_recv()
        p[...] += r[...]

    @pl.when(t >= 2)
    def _():
        to_prev.start()

    for owner in range(2):

        @pl.when(t == owner)
        def _():
            for k in range(nt - 1, -1, -1):
                if k != owner:
                    spread(owner, k).start()
            tot[owner] = p[...]

    saves[1].start()
    for owner in range(2):
        wait_in(t != owner, spread(owner, 0))
    grad_ref[...] = tot[0] + tot[1]
    save_grad = pltpu.make_async_copy(grad_ref, grad_hbm, o_sem.at[2])
    save_grad.start()

    @pl.when(t >= 2)
    def _():
        to_prev.wait_send()

    for owner in range(2):

        @pl.when(t == owner)
        def _():
            for k in range(nt):
                if k != owner:
                    spread(owner, k).wait_send()

    @pl.when(t > 0)
    def _():
        for copy in mains:
            copy.wait_send()

    for q, copy in first + second:
        wait_out(q[1], copy)
    for q, copy in around_m:
        wait_out(jnp.logical_and(last, q[1]), copy)
    for q, copy in down:
        wait_out(jnp.logical_and(t > 0, q[1]), copy)
    for save in saves:
        save.wait()
    save_grad.wait()


def shards(sources, forward_states, terminal, damping, contact_stiff, regions):
    nt, ns = lax.axis_size("tm"), lax.axis_size("sx")
    steps, bx, by, cz = sources.shape
    assert nt > 2 and steps == 2 and bx == BLOCK_CELLS and lax.axis_size("sy") == 2
    hbm = pl.BlockSpec(memory_space=pltpu.HBM)
    f32 = jnp.float32
    ext = (bx + 2 * H, by + HY, cz)
    block = (bx, by, cz)
    dma = pltpu.SemaphoreType.DMA
    return pl.pallas_call(
        functools.partial(kernel, nt, ns),
        out_shape=(
            jax.ShapeDtypeStruct(sources.shape, f32),
            jax.ShapeDtypeStruct(block, f32),
        ),
        in_specs=[hbm] * 6,
        out_specs=(hbm, hbm),
        scratch_shapes=[
            pltpu.VMEM(sources.shape, f32),
            pltpu.VMEM(block, f32),
            pltpu.VMEM(sources.shape, f32),
            pltpu.VMEM(sources.shape, f32),
            pltpu.SMEM(contact_stiff.shape, f32),
            pltpu.SMEM(regions.shape, jnp.int32),
            pltpu.VMEM((6, 8, cz), f32),
            pltpu.VMEM((2,) + ext, f32),
            pltpu.VMEM((2,) + ext, f32),
            pltpu.VMEM(ext, f32),
            pltpu.VMEM(ext, f32),
            pltpu.VMEM(ext, f32),
            pltpu.VMEM(block, f32),
            pltpu.VMEM(block, f32),
            pltpu.VMEM(block, f32),
            pltpu.VMEM((2,) + block, f32),
            dma((6,)), dma((3,)), dma((5,)), dma((5,)), dma((5,)), dma((5,)), dma((5,)),
            dma((13,)), dma((13,)), dma((1,)), dma((1,)), dma((nt,)), dma((2,)),
        ],
        compiler_params=pltpu.CompilerParams(
            collective_id=0, has_side_effects=True, vmem_limit_bytes=64 * 1024 * 1024
        ),
    )(sources, forward_states, terminal, damping, contact_stiff, regions)


def solution(mesh):
    in_specs = (
        P("tm", "sx", "sy", None),
        P("tm", "sx", "sy", None),
        P("sx", "sy", None),
        P("sx", "sy", None),
        P(),
        P("tm", "sx", "sy"),
    )
    out_specs = (P("tm", "sx", "sy", None), P("sx", "sy", None))
    return jax.shard_map(shards, mesh=mesh, in_specs=in_specs, out_specs=out_specs, check_vma=False)
```
